32 devices in a mesh: groups: 2 (over y), blk: 4 (over z), heads: 2 (over x), sub: 2 (over core).
Axes of the slice: x: 2, y: 2, z: 4, core: 2. Of those that a mesh axis runs over, the one named last changes fastest.
Arguments:
- patches: bfloat16 [1024, 1024], P(('groups', 'blk')), parts along dimension 0, may hold values from -6 to 6
- conv_taps: float32 [3, 1024], replicated, may hold values from -3 to 3
- w_query: bfloat16 [1024, 1024], P(None, ('heads', 'sub')), may hold values from -0.1875 to 0.1875
- w_key: bfloat16 [1024, 1024], P(None, ('heads', 'sub')), may hold values from -0.1875 to 0.1875
- w_value: bfloat16 [1024, 1024], P(None, ('heads', 'sub')), may hold values from -0.1875 to 0.1875
- w_output: bfloat16 [1024, 1024], P(None, ('heads', 'sub')), may hold values from -0.1875 to 0.1875
- tile_mask: int32 [8, 4], P('groups'), parts along dimension 0, may hold values from 0 to 1, as said below
- cotangent: bfloat16 [1024, 1024], P(('groups', 'blk'), ('heads', 'sub')), parts along dimension 0, may hold values from -6 to 6
Outputs:
- input_grad: float32 [1024, 1024], P(('groups', 'blk'), ('heads', 'sub')), parts along dimension 0
- conv_grad: float32 [6, 1024], P('groups', ('heads', 'sub')), parts along dimension 0
- grad_query: float32 [2048, 1024], P(('groups', 'blk'), ('heads', 'sub')), parts along dimension 0
- grad_key: float32 [2048, 1024], P(('groups', 'blk'), ('heads', 'sub')), parts along dimension 0
- grad_value: float32 [2048, 1024], P(('groups', 'blk'), ('heads', 'sub')), parts along dimension 0
- grad_output: float32 [2048, 1024], P(('groups', 'blk'), ('heads', 'sub')), parts along dimension 0
The draws below stay inside these ranges and needn't reach their ends.
There are 2 independent parts, one for each index of `groups`. The reference program is written for one: setup_inputs(seed, part) draws one part's arguments, and reference() takes and returns one part's arrays. A program takes and returns all parts, laid end to end along the dimension named above; an argument that names none is the same for every part. Nothing has to cross between parts.
Inputs may be any that keep to these rules, and one draw needn't show every extreme that they name: tile_mask[i][i] is 1 for every tile and tile_mask is symmetric.
All inputs are finite; a program needn't handle non-finite values.
Results may differ from the reference program's by a relative error of at most 0.004.
The reference program's roundings to bfloat16 on the way count: a program that leaves them out, or rounds other values in their place, can miss the bound.
Values may be sent and summed in bfloat16 or wider, within the bound.
A program may use at most 64 MiB of HBM per device.

```python
import jax
import jax.numpy as jnp
from jax import lax

D = 1024
HEADS = 16
TILE = 128
TOKENS = 512


def draw_tile_mask(key, part):
    count = TOKENS // TILE
    first_key, second_key = jax.random.split(jax.random.fold_in(key, 17))
    limits = jax.random.randint(first_key, (count, 1), 1, 40)
    rolls = jax.random.randint(second_key, (count, count), 0, 100)
    picked = rolls < limits
    places = jnp.arange(count, dtype=jnp.int32)
    band = jnp.abs(places[:, None] - places[None, :]) <= 1
    return (band | picked | picked.T).astype(jnp.int32)


def shard_levels(stream_key, shape, shards, low, high):
    def one(axis_at, shards_of):
        steps = jax.random.uniform(jax.random.fold_in(jax.random.fold_in(stream_key, 6), axis_at), (shards_of,), jnp.float32, low / len(shards), high / len(shards))
        return jnp.repeat(jnp.exp(steps), shape[axis_at] // shards_of).reshape((-1,) + (1,) * (len(shape) - axis_at - 1))

    factor_of = one(*shards[0])
    for cut in shards[1:]:
        factor_of = factor_of * one(*cut)
    return factor_of


def noise(rng, shape, width, most, pieces=(), kind=jnp.bfloat16):
    level = shard_levels(rng, shape, pieces, -0.22, 0.18) if pieces else 1.0
    array = jax.random.normal(rng, shape, jnp.float32) * width * level
    return jnp.minimum(jnp.maximum(array, -most), most).astype(kind)


def setup_inputs(seed: int = 0, part: int = 0) -> dict:
    key_of = jax.random.split(jax.random.key(seed), 9)
    part_splits = jax.random.split(jax.random.fold_in(key_of[8], part), 9)
    return {
        "patches": noise(part_splits[0], (TOKENS, D), 1.0, 6.0, ((0, 4),)),
        "conv_taps": noise(key_of[1], (3, D), 0.4, 3.0, (), jnp.float32),
        "w_query": noise(key_of[2], (D, D), D ** -0.5, 0.1875, ((1, 4),)),
        "w_key": noise(key_of[3], (D, D), D ** -0.5, 0.1875, ((1, 4),)),
        "w_value": noise(key_of[4], (D, D), D ** -0.5, 0.1875, ((1, 4),)),
        "w_output": noise(key_of[5], (D, D), D ** -0.5, 0.1875, ((1, 4),)),
        "tile_mask": draw_tile_mask(jax.random.fold_in(jax.random.fold_in(key_of[8], part), 71), part),
        "cotangent": noise(part_splits[7], (TOKENS, D), 1.0, 6.0, ((0, 4), (1, 4))),
    }


def reference(patches, conv_taps, w_query, w_key, w_value, w_output, tile_mask, cotangent):
    head_size = D // HEADS
    scale = head_size ** -0.5
    norm = TOKENS ** -0.5
    plain = patches.astype(jnp.float32)
    padded = jnp.pad(plain, ((1, 1), (0, 0)))
    mixed = (plain + conv_taps[0] * padded[:-2] + conv_taps[1] * plain + conv_taps[2] * padded[2:]).astype(jnp.bfloat16)
    queries = jnp.dot(mixed, w_query, preferred_element_type=jnp.float32).astype(jnp.bfloat16)
    keys = jnp.dot(mixed, w_key, preferred_element_type=jnp.float32).astype(jnp.bfloat16)
    values = jnp.dot(mixed, w_value, preferred_element_type=jnp.float32).astype(jnp.bfloat16)
    grad_att = jnp.dot(cotangent, w_output, preferred_element_type=jnp.float32).astype(jnp.bfloat16)
    mask_f = tile_mask.astype(jnp.float32)
    key_tiles = jnp.arange(TOKENS, dtype=jnp.int32) // TILE
    block = 512 if TOKENS % 512 == 0 else TILE
    nblocks = TOKENS // block

    def one_head(head):
        first = (head * head_size).astype(jnp.int32)
        query_h = lax.dynamic_slice_in_dim(queries, first, head_size, 1)
        key_h = lax.dynamic_slice_in_dim(keys, first, head_size, 1)
        value_h = lax.dynamic_slice_in_dim(values, first, head_size, 1)
        grad_h = lax.dynamic_slice_in_dim(grad_att, first, head_size, 1)

        def step(carry, index):
            acc_k, acc_v = carry
            lower = (index * block).astype(jnp.int32)
            query_b = lax.dynamic_slice_in_dim(query_h, lower, block, 0)
            grad_b = lax.dynamic_slice_in_dim(grad_h, lower, block, 0)
            row_tiles = (lower + jnp.arange(block, dtype=jnp.int32)) // TILE
            allowed = mask_f[row_tiles][:, key_tiles] > 0.5
            score = jnp.dot(query_b, key_h.T, preferred_element_type=jnp.float32) * scale
            weight = jnp.where(allowed, jnp.exp(jnp.where(allowed, score, 0.0)), 0.0)
            total = jnp.sum(weight, -1, keepdims=True)
            att32 = jnp.dot(weight.astype(jnp.bfloat16), value_h, preferred_element_type=jnp.float32) / total
            delta = jnp.sum(grad_b.astype(jnp.float32) * att32, -1, keepdims=True)
            prob = weight / total
            dprob = jnp.dot(grad_b, value_h.T, preferred_element_type=jnp.float32)
            dscore = (prob * (dprob - delta) * scale).astype(jnp.bfloat16)
            grad_qb = jnp.dot(dscore, key_h, preferred_element_type=jnp.float32).astype(jnp.bfloat16)
            acc_k = acc_k + jnp.dot(dscore.T, query_b, preferred_element_type=jnp.float32)
            acc_v = acc_v + jnp.dot(prob.astype(jnp.bfloat16).T, grad_b, preferred_element_type=jnp.float32)
            return (acc_k, acc_v), (att32.astype(jnp.bfloat16), grad_qb)

        zeros = jnp.zeros((TOKENS, head_size), jnp.float32)
        (acc_k, acc_v), (att_blocks, grad_blocks) = lax.scan(step, (zeros, zeros), jnp.arange(nblocks, dtype=jnp.int32))
        return (att_blocks.reshape(TOKENS, head_size), grad_blocks.reshape(TOKENS, head_size),
                acc_k.astype(jnp.bfloat16), acc_v.astype(jnp.bfloat16))

    att_all, grad_q, grad_k, grad_v = lax.map(one_head, jnp.arange(HEADS, dtype=jnp.int32))

    def side_by_side(stacked):
        return jnp.transpose(stacked, (1, 0, 2)).reshape(TOKENS, D)

    attended = side_by_side(att_all)
    grad_q = side_by_side(grad_q)
    grad_k = side_by_side(grad_k)
    grad_v = side_by_side(grad_v)
    grad_query = jnp.dot(mixed.T, grad_q, preferred_element_type=jnp.float32) * norm
    grad_key = jnp.dot(mixed.T, grad_k, preferred_element_type=jnp.float32) * norm
    grad_value = jnp.dot(mixed.T, grad_v, preferred_element_type=jnp.float32) * norm
    grad_output = jnp.dot(cotangent.T, attended, preferred_element_type=jnp.float32) * norm
    branch = (jnp.dot(grad_q, w_query.T, preferred_element_type=jnp.float32)
              + jnp.dot(grad_k, w_key.T, preferred_element_type=jnp.float32)
              + jnp.dot(grad_v, w_value.T, preferred_element_type=jnp.float32))
    grad_mixed = cotangent.astype(jnp.float32) + branch
    padded_grad = jnp.pad(grad_mixed, ((1, 1), (0, 0)))
    input_grad = grad_mixed * (1.0 + conv_taps[1]) + conv_taps[0] * padded_grad[2:] + conv_taps[2] * padded_grad[:-2]
    conv_grad = jnp.stack([jnp.sum(grad_mixed * padded[:-2], 0), jnp.sum(grad_mixed * plain, 0),
                           jnp.sum(grad_mixed * padded[2:], 0)]) * norm
    return input_grad, conv_grad, grad_query, grad_key, grad_value, grad_output
```

```python
import functools

import jax
import jax.numpy as jnp
from jax import lax
from jax.experimental import pallas as pl
from jax.experimental.pallas import tpu as pltpu
from jax.sharding import PartitionSpec as P

D = 1024
HEADS = 16
TILE = 128


def padded(cells, sides, width):
    for axis, dim in sides:
        count = lax.axis_size(axis)
        ends = count - 1
        head = lax.slice_in_dim(cells, 0, width, axis=dim)
        tail = lax.slice_in_dim(cells, cells.shape[dim] - width, cells.shape[dim], axis=dim)
        cells = jnp.concatenate(
            [
                lax.ppermute(tail, axis, [(i, (i + 1) % count) for i in range(ends)]),
                cells,
                lax.ppermute(head, axis, [((i + 1) % count, i) for i in range(ends)]),
            ],
            axis=dim,
        )
    return cells


def from_behind(value, axis, steps):
    count = lax.axis_size(axis)
    pairs = [(source, (source + steps) % count) for source in range(count)]
    return lax.ppermute(value, axis, pairs)


def allowed_rows(mask_bf, first_query, query_count, first_key, key_count):
    tiles = mask_bf.shape[0]
    columns = jnp.arange(tiles, dtype=jnp.int32)
    query_tiles = (first_query + jnp.arange(query_count, dtype=jnp.int32)) // TILE
    key_tiles = (first_key + jnp.arange(key_count, dtype=jnp.int32)) // TILE
    query_hot = (query_tiles[:, None] == columns[None, :]).astype(jnp.bfloat16)
    key_hot = (key_tiles[:, None] == columns[None, :]).astype(jnp.bfloat16)
    picked = jnp.dot(query_hot, mask_bf, preferred_element_type=jnp.float32).astype(jnp.bfloat16)
    return jnp.einsum("qn,kn->qk", picked, key_hot, preferred_element_type=jnp.float32) > 0.5


def per_device(patches, conv_taps, w_query, w_key, w_value, w_output, tile_mask, cotangent):
    rows = patches.shape[0]
    local = w_query.shape[1]
    head_size = D // HEADS
    heads_here = local // head_size
    cycle_size = lax.axis_size("blk")
    position = lax.axis_index("blk")
    total_rows = rows * cycle_size
    scale = head_size ** (-0.5)
    norm = total_rows ** (-0.5)
    mask_bf = tile_mask.astype(jnp.bfloat16)
    first_query = position * rows
    padded_in = padded(patches, (("blk", 0),), 1)
    padded32 = padded_in.astype(jnp.float32)
    middle = padded32[1:-1]
    mixed = (
        middle + conv_taps[0] * padded32[:-2] + conv_taps[1] * middle + conv_taps[2] * padded32[2:]
    ).astype(jnp.bfloat16)
    queries = jnp.dot(mixed, w_query, preferred_element_type=jnp.float32).astype(jnp.bfloat16)
    keys_own = jnp.dot(mixed, w_key, preferred_element_type=jnp.float32).astype(jnp.bfloat16)
    values_own = jnp.dot(mixed, w_value, preferred_element_type=jnp.float32).astype(jnp.bfloat16)
    keys_all, values_all = (
        lax.all_gather(keys_own, "blk", axis=0, tiled=True),
        lax.all_gather(values_own, "blk", axis=0, tiled=True),
    )
    cot_full = lax.all_gather(cotangent, ("heads", "sub"), axis=1, tiled=True)
    grad_att = jnp.dot(cot_full, w_output, preferred_element_type=jnp.float32).astype(jnp.bfloat16)
    group = 1
    for power in range(12):
        if group * 2 * rows <= 1024 and cycle_size % (group * 2) == 0:
            group = group * 2
    span = group * rows
    blocks = cycle_size // group
    query_heads = queries.reshape(rows, heads_here, head_size)
    grad_heads = grad_att.reshape(rows, heads_here, head_size)
    key_blocks = keys_all.reshape(blocks, span, heads_here, head_size)
    value_blocks = values_all.reshape(blocks, span, heads_here, head_size)
    block_ids = jnp.arange(blocks, dtype=jnp.int32)

    def weights_of(key_block, allowed):
        raw = (
            jnp.einsum("qhd,khd->hqk", query_heads, key_block, preferred_element_type=jnp.float32)
            * scale
        )
        return jnp.where(allowed[None], jnp.exp(jnp.where(allowed[None], raw, 0.0)), 0.0)

    def forward_step(state, inputs):
        block_id, key_block, value_block = inputs
        allowed = allowed_rows(mask_bf, first_query, rows, block_id * span, span)
        accum, totals = state
        weights = weights_of(key_block, allowed)
        added = jnp.einsum(
            "hqk,khd->hqd",
            weights.astype(jnp.bfloat16),
            value_block,
            preferred_element_type=jnp.float32,
        )
        state = (accum + added, totals + jnp.sum(weights, -1))
        return (state, None)

    start_state = (
        jnp.zeros((heads_here, rows, head_size), jnp.float32),
        jnp.zeros((heads_here, rows), jnp.float32),
    )
    (accum, totals), unused = lax.scan(
        forward_step, start_state, (block_ids, key_blocks, value_blocks)
    )
    attended32 = accum / totals[:, :, None]
    attended = jnp.transpose(attended32, (1, 0, 2)).reshape(rows, local).astype(jnp.bfloat16)
    deltas = jnp.einsum("qhd,hqd->hq", grad_heads.astype(jnp.float32), attended32)

    def local_grads(key_block, value_block, allowed):
        weights = weights_of(key_block, allowed)
        probs = weights / totals[:, :, None]
        dprobs = jnp.einsum(
            "qhd,khd->hqk", grad_heads, value_block, preferred_element_type=jnp.float32
        )
        dscores = (probs * (dprobs - deltas[:, :, None]) * scale).astype(jnp.bfloat16)
        return (
            jnp.einsum("hqk,khd->qhd", dscores, key_block, preferred_element_type=jnp.float32),
            jnp.einsum("hqk,qhd->khd", dscores, query_heads, preferred_element_type=jnp.float32),
            jnp.einsum(
                "hqk,qhd->khd",
                probs.astype(jnp.bfloat16),
                grad_heads,
                preferred_element_type=jnp.float32,
            ),
        )

    def shard_grads(block):
        wrapped = jnp.remainder(block, cycle_size)
        key_block = lax.dynamic_slice_in_dim(keys_all, wrapped * rows, rows, 0).reshape(
            rows, heads_here, head_size
        )
        value_block = lax.dynamic_slice_in_dim(values_all, wrapped * rows, rows, 0).reshape(
            rows, heads_here, head_size
        )
        allowed = allowed_rows(mask_bf, first_query, rows, wrapped * rows, rows)
        query_add, key_term, value_term = local_grads(key_block, value_block, allowed)
        return (
            query_add,
            jnp.stack([key_term.reshape(rows, local), value_term.reshape(rows, local)]),
        )

    query_first, carried_first = shard_grads(position - 1)

    def turn(step, state):
        accum_q, carried = state
        moved = from_behind(carried, "blk", 1)
        query_add, term = shard_grads(position - step - 1)
        return (accum_q + query_add, moved + term)

    accum_q, summed = lax.fori_loop(1, cycle_size, turn, (query_first, carried_first))
    grad_keys = summed[0].astype(jnp.bfloat16)
    grad_values = summed[1].astype(jnp.bfloat16)
    grad_queries = accum_q.reshape(rows, local).astype(jnp.bfloat16)
    stacked = jnp.stack(
        [
            jnp.einsum("td,tc->dc", mixed, grad_queries, preferred_element_type=jnp.float32),
            jnp.einsum("td,tc->dc", mixed, grad_keys, preferred_element_type=jnp.float32),
            jnp.einsum("td,tc->dc", mixed, grad_values, preferred_element_type=jnp.float32),
            jnp.einsum("td,tc->dc", cot_full, attended, preferred_element_type=jnp.float32),
        ]
    )
    weight_sums = lax.psum_scatter(stacked, "blk", scatter_dimension=1, tiled=True) * norm
    partial_grad = (
        jnp.einsum("tc,dc->td", grad_queries, w_query, preferred_element_type=jnp.float32)
        + jnp.einsum("tc,dc->td", grad_keys, w_key, preferred_element_type=jnp.float32)
        + jnp.einsum("tc,dc->td", grad_values, w_value, preferred_element_type=jnp.float32)
    )
    grad_mixed = lax.psum_scatter(
        partial_grad, ("heads", "sub"), scatter_dimension=1, tiled=True
    ) + cotangent.astype(jnp.float32)
    columns_here = cotangent.shape[1]
    offset = lax.axis_index(("heads", "sub")) * columns_here
    taps_here = lax.dynamic_slice_in_dim(conv_taps, offset, columns_here, 1)
    padded_grad = padded(grad_mixed.astype(jnp.bfloat16), (("blk", 0),), 1).astype(grad_mixed.dtype)
    input_grad = (
        grad_mixed * (1.0 + taps_here[1])
        + taps_here[0] * padded_grad[2:]
        + taps_here[2] * padded_grad[:-2]
    )
    patch_cols = lax.dynamic_slice_in_dim(padded32, offset, columns_here, 1)
    conv_terms = jnp.stack(
        [
            jnp.sum(grad_mixed * patch_cols[:-2], 0),
            jnp.sum(grad_mixed * patch_cols[1:-1], 0),
            jnp.sum(grad_mixed * patch_cols[2:], 0),
        ]
    )
    conv_grad = lax.psum(conv_terms, "blk") * norm
    return (input_grad, conv_grad, weight_sums[0], weight_sums[1], weight_sums[2], weight_sums[3])

MESH = pl.DeviceIdType.MESH
BF = jnp.bfloat16
F32 = jnp.float32


def dot(a, b, ca, cb):
    return lax.dot_general(a, b, (((ca,), (cb,)), ((), ())), preferred_element_type=F32)


def fused(
    n, norm,
    patches, taps, w_query, w_key, w_value, w_output, mask, cot,
    out_in, out_conv, out_q, out_k, out_v, out_o,
    slabs, mixed, wq, wk, wv, wo, tp, acc, heads4, grads, att, acc_k, acc_v,
    back_out, back_in, wide_out, wide_in, part_out, part_in, edge_out, edge_in,
    sem_loc, sem_w, zs, zr, xs, xr, cs, cr, bs, br, gs, gr, ps, pr, es, er,
):
    g = lax.axis_index("groups")
    b = lax.axis_index("blk")
    x = lax.axis_index("heads")
    s = lax.axis_index("sub")
    h, hx, hc, hd = x * 2 + s, (1 - x) * 2 + s, x * 2 + 1 - s, (1 - x) * 2 + 1 - s
    rows = patches.shape[0]
    wide = cot.shape[1]
    half = wide // 2
    hs = D // HEADS
    scale = hs ** (-0.5)
    peers = [lax.rem(b + k, n) for k in range(1, n)]
    at_peer = [(g, p, x, s) for p in peers]
    at_x, at_c, at_d = (g, b, 1 - x, s), (g, b, x, 1 - s), (g, b, 1 - x, 1 - s)

    def send(src, dst, ss, rs, where):
        c = pltpu.make_async_remote_copy(
            src_ref=src, dst_ref=dst, send_sem=ss, recv_sem=rs, device_id=where, device_id_type=MESH
        )
        c.start()
        return c

    def got(ref, sem):
        pltpu.make_async_remote_copy(
            src_ref=ref, dst_ref=ref, send_sem=sem, recv_sem=sem, device_id=at_x, device_id_type=MESH
        ).wait_recv()

    locals_ = []
    for c in range(4):
        locals_.append(
            pltpu.make_async_copy(
                patches.at[:, pl.ds(c * wide, wide)], slabs.at[b, c, 0], sem_loc.at[c]
            )
        )
    locals_.append(pltpu.make_async_copy(cot, slabs.at[b, h, 1], sem_loc.at[4]))
    locals_.append(pltpu.make_async_copy(taps, tp, sem_loc.at[5]))
    weights = [
        pltpu.make_async_copy(src, dst, sem_w.at[i])
        for i, (src, dst) in enumerate(((w_query, wq), (w_key, wk), (w_value, wv), (w_output, wo)))
    ]
    for c in locals_ + weights:
        c.start()
    barrier = pltpu.get_barrier_semaphore()
    for where in at_peer + [at_x, at_c, at_d]:
        pl.semaphore_signal(barrier, inc=1, device_id=where, device_id_type=MESH)
    pl.semaphore_wait(barrier, n + 2)

    sent = []
    own_cols = pl.ds(pl.multiple_of(h * wide, wide), wide)
    for k, where in enumerate(at_peer):
        sent.append(send(patches.at[:, own_cols], slabs.at[b, h, 0], zs.at[0, k], zr.at[0, b], where))
        sent.append(send(cot, slabs.at[b, h, 1], zs.at[1, k], zr.at[1, b], where))
    sent.append(send(cot, slabs.at[b, h, 1], xs.at[0], xr.at[b], at_x))
    sent.append(send(cot, slabs.at[b, h, 1], cs.at[0, 0], cr.at[0, b], at_c))
    for k, p in enumerate(peers):
        got(slabs.at[p, h, 0], zr.at[0, p])
        got(slabs.at[p, h, 1], zr.at[1, p])
        sent.append(send(slabs.at[p, h], slabs.at[p, h], xs.at[k + 1], xr.at[p], at_x))
        sent.append(send(slabs.at[p, h], slabs.at[p, h], cs.at[0, k + 1], cr.at[0, p], at_c))
    for c in locals_ + weights:
        c.wait()

    pair = pl.ds(pl.multiple_of((b // 2) * half, half), half)
    acc[...] = jnp.zeros_like(acc)
    row_of = lax.broadcasted_iota(jnp.int32, (n * rows, wide), 0)

    def quarter(c):
        cols = pl.ds(pl.multiple_of(c * wide, wide), wide)
        plain = slabs[:, c, 0].reshape(n * rows, wide).astype(F32)
        before = jnp.where(row_of == 0, 0.0, pltpu.roll(plain, 1, 0))
        after = jnp.where(row_of == n * rows - 1, 0.0, pltpu.roll(plain, n * rows - 1, 0))
        t = tp[:, cols]
        m = (plain + t[0:1] * before + t[1:2] * plain + t[2:3] * after).astype(BF)
        mixed[c] = m
        cq = slabs[:, c, 1].reshape(n * rows, wide)
        acc[0] += dot(m, wq[cols, pair], 1, 0)
        acc[1] += dot(m, wk[cols, pair], 1, 0)
        acc[2] += dot(m, wv[cols, pair], 1, 0)
        acc[3] += dot(cq, wo[cols, pair], 1, 0)

    quarter(h)
    got(slabs.at[b, hx, 1], xr.at[b])
    sent.append(send(slabs.at[b, hx, 1], slabs.at[b, hx, 1], cs.at[1, 0], cr.at[1, b], at_c))
    for k, p in enumerate(peers):
        got(slabs.at[p, hx], xr.at[p])
        sent.append(send(slabs.at[p, hx], slabs.at[p, hx], cs.at[1, k + 1], cr.at[1, p], at_c))
    quarter(hx)
    got(slabs.at[b, hc, 1], cr.at[0, b])
    for p in peers:
        got(slabs.at[p, hc], cr.at[0, p])
    quarter(hc)
    got(slabs.at[b, hd, 1], cr.at[1, b])
    for p in peers:
        got(slabs.at[p, hd], cr.at[1, p])
    quarter(hd)

    odd = lax.rem(b, 2) == 1
    for i in range(4):
        full = acc[i]
        heads4[i] = jnp.where(odd, pltpu.roll(full, hs, 1), full)[:, :hs].astype(BF)

    acc_k[...] = jnp.zeros_like(acc_k)
    acc_v[...] = jnp.zeros_like(acc_v)
    keys, values = heads4[1], heads4[2]
    for i in range(n):
        here = pl.ds(i * rows, rows)
        query, grad = heads4[0, here, :], heads4[3, here, :]
        allowed = (
            jnp.concatenate([jnp.full((rows, TILE), mask[i, j], jnp.int32) for j in range(n)], axis=1)
            == 1
        )
        score = dot(query, keys, 1, 1) * scale
        weight = jnp.where(allowed, jnp.exp(jnp.where(allowed, score, 0.0)), 0.0)
        inverse = 1.0 / jnp.sum(weight, -1, keepdims=True)
        att32 = dot(weight.astype(BF), values, 1, 0) * inverse
        delta = jnp.sum(grad.astype(F32) * att32, -1, keepdims=True)
        prob = weight * inverse
        dprob = dot(grad, values, 1, 1)
        dscore = (prob * (dprob - delta) * scale).astype(BF)
        att[here, :] = att32.astype(BF)
        grads[here, 0:hs] = dot(dscore, keys, 1, 0).astype(BF)
        acc_k[...] += dot(dscore, query, 0, 0)
        acc_v[...] += dot(prob.astype(BF), grad, 0, 0)
    grads[:, hs : 2 * hs] = acc_k[...].astype(BF)
    grads[:, 2 * hs : 3 * hs] = acc_v[...].astype(BF)

    def packed(t):
        base = pl.multiple_of(t * rows, rows)
        both = grads[pl.ds(base, rows), 0 : 2 * hs]
        third = grads[pl.ds(base, rows), 2 * hs : 3 * hs]
        return both, jnp.concatenate([third[: rows // 2], third[rows // 2 :]], axis=1)

    for k, p in enumerate(peers):
        both, third = packed(p)
        back_out[k, :rows] = both
        back_out[k, rows:] = third
        sent.append(send(back_out.at[k], back_in.at[b], bs.at[k], br.at[b], at_peer[k]))
    both, third = packed(b)
    back_in[b, :rows] = both
    back_in[b, rows:] = third

    three = grads[...]
    attended = att[...]

    def weight_grads(c):
        m = dot(mixed[c], three, 0, 0) * norm
        o = dot(slabs[:, c, 1].reshape(n * rows, wide), attended, 0, 0) * norm
        first = m[:, : 2 * hs].astype(BF)
        return first, jnp.concatenate([m[:, 2 * hs :], o], axis=1).astype(BF)

    for k, p in enumerate(peers):
        first, second = weight_grads(p)
        wide_out[k, 0] = first
        wide_out[k, 1] = second
        sent.append(send(wide_out.at[k], wide_in.at[b], gs.at[k], gr.at[b], at_peer[k]))
    first, second = weight_grads(b)
    wide_in[b, 0] = first
    wide_in[b, 1] = second

    for p in peers:
        got(back_in.at[p], br.at[p])
    grad_q = jnp.concatenate([back_in[j, :rows, :hs] for j in range(n)], axis=1)
    grad_k = jnp.concatenate([back_in[j, :rows, hs:] for j in range(n)], axis=1)
    grad_v = jnp.concatenate(
        [
            jnp.concatenate([back_in[j, rows:, :hs] for j in range(n)], axis=1),
            jnp.concatenate([back_in[j, rows:, hs:] for j in range(n)], axis=1),
        ],
        axis=0,
    )

    def branch(c):
        cols = pl.ds(pl.multiple_of(c * wide, wide), wide)
        return (
            dot(grad_q, wq[cols, :], 1, 1) + dot(grad_k, wk[cols, :], 1, 1)
            + dot(grad_v, wv[cols, :], 1, 1)
        )

    for k, (c, where) in enumerate(((hx, at_x), (hd, at_d), (hc, at_c))):
        part_out[k] = branch(c).astype(BF)
        sent.append(send(part_out.at[k], part_in.at[k], ps.at[k], pr.at[k], where))
    total = branch(h) + slabs[b, h, 1].astype(F32)
    for k in range(3):
        got(part_in.at[k], pr.at[k])
        total = total + part_in[k].astype(F32)

    first_row = lax.broadcasted_iota(jnp.int32, (rows, wide), 0) == 0
    last_row = lax.broadcasted_iota(jnp.int32, (rows, wide), 0) == rows - 1
    low, high = lax.rem(b + n - 1, n), lax.rem(b + 1, n)
    plain = slabs[b, h, 0].astype(F32)
    edge_low = jnp.where(b > 0, slabs[low, h, 0, rows - 16 :].astype(F32)[15:16], 0.0)
    edge_high = jnp.where(b < n - 1, slabs[high, h, 0, :16].astype(F32)[0:1], 0.0)
    before = jnp.where(first_row, edge_low, pltpu.roll(plain, 1, 0))
    after = jnp.where(last_row, edge_high, pltpu.roll(plain, rows - 1, 0))
    edge_out[0:1] = jnp.sum(total * before, 0, keepdims=True)
    edge_out[1:2] = jnp.sum(total * plain, 0, keepdims=True)
    edge_out[2:3] = jnp.sum(total * after, 0, keepdims=True)
    edge_out[3:4] = total[0:1]
    edge_out[4:5] = total[rows - 1 :]
    edge_out[5:8] = jnp.zeros((3, wide), F32)
    for k, where in enumerate(at_peer):
        sent.append(send(edge_out, edge_in.at[b], es.at[k], er.at[b], where))
    edge_in[b] = edge_out[...]

    for p in peers:
        got(wide_in.at[p], gr.at[p])
    for slot, side, out in ((0, 0, out_q), (0, 1, out_k), (1, 0, out_v), (1, 1, out_o)):
        out[...] = jnp.concatenate(
            [wide_in[j, slot, :, side * hs : (side + 1) * hs] for j in range(n)], axis=1
        ).astype(F32)
    for p in peers:
        got(edge_in.at[p], er.at[p])
    summed = edge_in[0]
    for j in range(1, n):
        summed = summed + edge_in[j]
    out_conv[...] = summed[0:3] * norm
    t = tp[:, own_cols]
    edge_low = jnp.where(b > 0, edge_in[low][4:5], 0.0)
    edge_high = jnp.where(b < n - 1, edge_in[high][3:4], 0.0)
    before = jnp.where(first_row, edge_low, pltpu.roll(total, 1, 0))
    after = jnp.where(last_row, edge_high, pltpu.roll(total, rows - 1, 0))
    out_in[...] = total * (1.0 + t[1:2]) + t[0:1] * after + t[2:3] * before
    for c in sent:
        c.wait_send()


def fused_device(patches, conv_taps, w_query, w_key, w_value, w_output, tile_mask, cotangent):
    n = lax.axis_size("blk")
    rows, wide = cotangent.shape
    hs = D // HEADS
    tokens = n * rows
    dma = pltpu.SemaphoreType.DMA
    anywhere = pl.BlockSpec(memory_space=pl.ANY)
    return pl.pallas_call(
        functools.partial(fused, n, tokens ** (-0.5)),
        out_shape=(
            jax.ShapeDtypeStruct((rows, wide), F32),
            jax.ShapeDtypeStruct((3, wide), F32),
        )
        + (jax.ShapeDtypeStruct((D // n, wide), F32),) * 4,
        in_specs=[anywhere] * 6 + [pl.BlockSpec(memory_space=pltpu.SMEM), anywhere],
        out_specs=(pl.BlockSpec(memory_space=pltpu.VMEM),) * 6,
        scratch_shapes=[
            pltpu.VMEM((n, 4, 2, rows, wide), BF),
            pltpu.VMEM((4, tokens, wide), BF),
            pltpu.VMEM((D, wide), BF),
            pltpu.VMEM((D, wide), BF),
            pltpu.VMEM((D, wide), BF),
            pltpu.VMEM((D, wide), BF),
            pltpu.VMEM((3, D), F32),
            pltpu.VMEM((4, tokens, wide // 2), F32),
            pltpu.VMEM((4, tokens, hs), BF),
            pltpu.VMEM((tokens, 3 * hs), BF),
            pltpu.VMEM((tokens, hs), BF),
            pltpu.VMEM((tokens, hs), F32),
            pltpu.VMEM((tokens, hs), F32),
            pltpu.VMEM((n - 1, rows + rows // 2, 2 * hs), BF),
            pltpu.VMEM((n, rows + rows // 2, 2 * hs), BF),
            pltpu.VMEM((n - 1, 2, D // n, 2 * hs), BF),
            pltpu.VMEM((n, 2, D // n, 2 * hs), BF),
            pltpu.VMEM((3, rows, wide), BF),
            pltpu.VMEM((3, rows, wide), BF),
            pltpu.VMEM((8, wide), F32),
            pltpu.VMEM((n, 8, wide), F32),
            dma((6,)), dma((4,)),
            dma((2, n - 1)), dma((2, n)),
            dma((n,)), dma((n,)),
            dma((2, n)), dma((2, n)),
            dma((n - 1,)), dma((n,)),
            dma((n - 1,)), dma((n,)),
            dma((3,)), dma((3,)),
            dma((n - 1,)), dma((n,)),
        ],
        compiler_params=pltpu.CompilerParams(
            collective_id=0, has_side_effects=True, vmem_limit_bytes=48 * 1024 * 1024
        ),
    )(patches, conv_taps, w_query, w_key, w_value, w_output, tile_mask, cotangent)


def fits(mesh):
    shape = mesh.shape
    n = shape["blk"]
    return n == 4 and shape["heads"] == 2 and shape["sub"] == 2 and HEADS == 4 * n


def solution(mesh):
    in_specs = (
        P(("groups", "blk"), None),
        P(),
        P(None, ("heads", "sub")),
        P(None, ("heads", "sub")),
        P(None, ("heads", "sub")),
        P(None, ("heads", "sub")),
        P("groups", None),
        P(("groups", "blk"), ("heads", "sub")),
    )
    out_specs = (
        P(("groups", "blk"), ("heads", "sub")),
        P("groups", ("heads", "sub")),
        P(("groups", "blk"), ("heads", "sub")),
        P(("groups", "blk"), ("heads", "sub")),
        P(("groups", "blk"), ("heads", "sub")),
        P(("groups", "blk"), ("heads", "sub")),
    )
    return jax.shard_map(
        fused_device if fits(mesh) else per_device, mesh=mesh, in_specs=in_specs, out_specs=out_specs, check_vma=False
    )
```

```python
import functools

import jax
import jax.numpy as jnp
from jax import lax
from jax.experimental import pallas as pl
from jax.experimental.pallas import tpu as pltpu
from jax.sharding import PartitionSpec as P

D = 1024
HEADS = 16
TILE = 128


def padded(cells, sides, width):
    for axis, dim in sides:
        count = lax.axis_size(axis)
        ends = count - 1
        head = lax.slice_in_dim(cells, 0, width, axis=dim)
        tail = lax.slice_in_dim(cells, cells.shape[dim] - width, cells.shape[dim], axis=dim)
        cells = jnp.concatenate(
            [
                lax.ppermute(tail, axis, [(i, (i + 1) % count) for i in range(ends)]),
                cells,
                lax.ppermute(head, axis, [((i + 1) % count, i) for i in range(ends)]),
            ],
            axis=dim,
        )
    return cells


def from_behind(value, axis, steps):
    count = lax.axis_size(axis)
    pairs = [(source, (source + steps) % count) for source in range(count)]
    return lax.ppermute(value, axis, pairs)


def allowed_rows(mask_bf, first_query, query_count, first_key, key_count):
    tiles = mask_bf.shape[0]
    columns = jnp.arange(tiles, dtype=jnp.int32)
    query_tiles = (first_query + jnp.arange(query_count, dtype=jnp.int32)) // TILE
    key_tiles = (first_key + jnp.arange(key_count, dtype=jnp.int32)) // TILE
    query_hot = (query_tiles[:, None] == columns[None, :]).astype(jnp.bfloat16)
    key_hot = (key_tiles[:, None] == columns[None, :]).astype(jnp.bfloat16)
    picked = jnp.dot(query_hot, mask_bf, preferred_element_type=jnp.float32).astype(jnp.bfloat16)
    return jnp.einsum("qn,kn->qk", picked, key_hot, preferred_element_type=jnp.float32) > 0.5


def per_device(patches, conv_taps, w_query, w_key, w_value, w_output, tile_mask, cotangent):
    rows = patches.shape[0]
    local = w_query.shape[1]
    head_size = D // HEADS
    heads_here = local // head_size
    cycle_size = lax.axis_size("blk")
    position = lax.axis_index("blk")
    total_rows = rows * cycle_size
    scale = head_size ** (-0.5)
    norm = total_rows ** (-0.5)
    mask_bf = tile_mask.astype(jnp.bfloat16)
    first_query = position * rows
    padded_in = padded(patches, (("blk", 0),), 1)
    padded32 = padded_in.astype(jnp.float32)
    middle = padded32[1:-1]
    mixed = (
        middle + conv_taps[0] * padded32[:-2] + conv_taps[1] * middle + conv_taps[2] * padded32[2:]
    ).astype(jnp.bfloat16)
    queries = jnp.dot(mixed, w_query, preferred_element_type=jnp.float32).astype(jnp.bfloat16)
    keys_own = jnp.dot(mixed, w_key, preferred_element_type=jnp.float32).astype(jnp.bfloat16)
    values_own = jnp.dot(mixed, w_value, preferred_element_type=jnp.float32).astype(jnp.bfloat16)
    keys_all, values_all = (
        lax.all_gather(keys_own, "blk", axis=0, tiled=True),
        lax.all_gather(values_own, "blk", axis=0, tiled=True),
    )
    cot_full = lax.all_gather(cotangent, ("heads", "sub"), axis=1, tiled=True)
    grad_att = jnp.dot(cot_full, w_output, preferred_element_type=jnp.float32).astype(jnp.bfloat16)
    group = 1
    for power in range(12):
        if group * 2 * rows <= 1024 and cycle_size % (group * 2) == 0:
            group = group * 2
    span = group * rows
    blocks = cycle_size // group
    query_heads = queries.reshape(rows, heads_here, head_size)
    grad_heads = grad_att.reshape(rows, heads_here, head_size)
    key_blocks = keys_all.reshape(blocks, span, heads_here, head_size)
    value_blocks = values_all.reshape(blocks, span, heads_here, head_size)
    block_ids = jnp.arange(blocks, dtype=jnp.int32)

    def weights_of(key_block, allowed):
        raw = (
            jnp.einsum("qhd,khd->hqk", query_heads, key_block, preferred_element_type=jnp.float32)
            * scale
        )
        return jnp.where(allowed[None], jnp.exp(jnp.where(allowed[None], raw, 0.0)), 0.0)

    def forward_step(state, inputs):
        block_id, key_block, value_block = inputs
        allowed = allowed_rows(mask_bf, first_query, rows, block_id * span, span)
        accum, totals = state
        weights = weights_of(key_block, allowed)
        added = jnp.einsum(
            "hqk,khd->hqd",
            weights.astype(jnp.bfloat16),
            value_block,
            preferred_element_type=jnp.float32,
        )
        state = (accum + added, totals + jnp.sum(weights, -1))
        return (state, None)

    start_state = (
        jnp.zeros((heads_here, rows, head_size), jnp.float32),
        jnp.zeros((heads_here, rows), jnp.float32),
    )
    (accum, totals), unused = lax.scan(
        forward_step, start_state, (block_ids, key_blocks, value_blocks)
    )
    attended32 = accum / totals[:, :, None]
    attended = jnp.transpose(attended32, (1, 0, 2)).reshape(rows, local).astype(jnp.bfloat16)
    deltas = jnp.einsum("qhd,hqd->hq", grad_heads.astype(jnp.float32), attended32)

    def local_grads(key_block, value_block, allowed):
        weights = weights_of(key_block, allowed)
        probs = weights / totals[:, :, None]
        dprobs = jnp.einsum(
            "qhd,khd->hqk", grad_heads, value_block, preferred_element_type=jnp.float32
        )
        dscores = (probs * (dprobs - deltas[:, :, None]) * scale).astype(jnp.bfloat16)
        return (
            jnp.einsum("hqk,khd->qhd", dscores, key_block, preferred_element_type=jnp.float32),
            jnp.einsum("hqk,qhd->khd", dscores, query_heads, preferred_element_type=jnp.float32),
            jnp.einsum(
                "hqk,qhd->khd",
                probs.astype(jnp.bfloat16),
                grad_heads,
                preferred_element_type=jnp.float32,
            ),
        )

    def shard_grads(block):
        wrapped = jnp.remainder(block, cycle_size)
        key_block = lax.dynamic_slice_in_dim(keys_all, wrapped * rows, rows, 0).reshape(
            rows, heads_here, head_size
        )
        value_block = lax.dynamic_slice_in_dim(values_all, wrapped * rows, rows, 0).reshape(
            rows, heads_here, head_size
        )
        allowed = allowed_rows(mask_bf, first_query, rows, wrapped * rows, rows)
        query_add, key_term, value_term = local_grads(key_block, value_block, allowed)
        return (
            query_add,
            jnp.stack([key_term.reshape(rows, local), value_term.reshape(rows, local)]),
        )

    query_first, carried_first = shard_grads(position - 1)

    def turn(step, state):
        accum_q, carried = state
        moved = from_behind(carried, "blk", 1)
        query_add, term = shard_grads(position - step - 1)
        return (accum_q + query_add, moved + term)

    accum_q, summed = lax.fori_loop(1, cycle_size, turn, (query_first, carried_first))
    grad_keys = summed[0].astype(jnp.bfloat16)
    grad_values = summed[1].astype(jnp.bfloat16)
    grad_queries = accum_q.reshape(rows, local).astype(jnp.bfloat16)
    stacked = jnp.stack(
        [
            jnp.einsum("td,tc->dc", mixed, grad_queries, preferred_element_type=jnp.float32),
            jnp.einsum("td,tc->dc", mixed, grad_keys, preferred_element_type=jnp.float32),
            jnp.einsum("td,tc->dc", mixed, grad_values, preferred_element_type=jnp.float32),
            jnp.einsum("td,tc->dc", cot_full, attended, preferred_element_type=jnp.float32),
        ]
    )
    weight_sums = lax.psum_scatter(stacked, "blk", scatter_dimension=1, tiled=True) * norm
    partial_grad = (
        jnp.einsum("tc,dc->td", grad_queries, w_query, preferred_element_type=jnp.float32)
        + jnp.einsum("tc,dc->td", grad_keys, w_key, preferred_element_type=jnp.float32)
        + jnp.einsum("tc,dc->td", grad_values, w_value, preferred_element_type=jnp.float32)
    )
    grad_mixed = lax.psum_scatter(
        partial_grad, ("heads", "sub"), scatter_dimension=1, tiled=True
    ) + cotangent.astype(jnp.float32)
    columns_here = cotangent.shape[1]
    offset = lax.axis_index(("heads", "sub")) * columns_here
    taps_here = lax.dynamic_slice_in_dim(conv_taps, offset, columns_here, 1)
    padded_grad = padded(grad_mixed.astype(jnp.bfloat16), (("blk", 0),), 1).astype(grad_mixed.dtype)
    input_grad = (
        grad_mixed * (1.0 + taps_here[1])
        + taps_here[0] * padded_grad[2:]
        + taps_here[2] * padded_grad[:-2]
    )
    patch_cols = lax.dynamic_slice_in_dim(padded32, offset, columns_here, 1)
    conv_terms = jnp.stack(
        [
            jnp.sum(grad_mixed * patch_cols[:-2], 0),
            jnp.sum(grad_mixed * patch_cols[1:-1], 0),
            jnp.sum(grad_mixed * patch_cols[2:], 0),
        ]
    )
    conv_grad = lax.psum(conv_terms, "blk") * norm
    return (input_grad, conv_grad, weight_sums[0], weight_sums[1], weight_sums[2], weight_sums[3])

MESH = pl.DeviceIdType.MESH
BF = jnp.bfloat16
F32 = jnp.float32


def dot(a, b, ca, cb):
    return lax.dot_general(a, b, (((ca,), (cb,)), ((), ())), preferred_element_type=F32)


def fused(
    n, norm,
    patches, taps, w_query, w_key, w_value, w_output, mask_in, cot,
    out_in, out_conv, out_q, out_k, out_v, out_o,
    mask, slabs, mixed, wq, wk, wv, wo, tp, acc, heads4, grads, probs, dscores, held,
    part_out, part_in, edge_out, edge_in,
    sem_loc, sem_w, zs, zr, xs, xr, cs, cr, ps, pr, es, er,
):
    g = lax.axis_index("groups")
    b = lax.axis_index("blk")
    x = lax.axis_index("heads")
    s = lax.axis_index("sub")
    h, hx, hc, hd = x * 2 + s, (1 - x) * 2 + s, x * 2 + 1 - s, (1 - x) * 2 + 1 - s
    rows = patches.shape[0]
    wide = cot.shape[1]
    local = wide // (D // HEADS)
    hs = D // HEADS
    scale = hs ** (-0.5)
    peers = [lax.rem(b + k, n) for k in range(1, n)]
    at_peer = [(g, p, x, s) for p in peers]
    at_x, at_c, at_d = (g, b, 1 - x, s), (g, b, x, 1 - s), (g, b, 1 - x, 1 - s)

    def send(src, dst, ss, rs, where):
        c = pltpu.make_async_remote_copy(
            src_ref=src, dst_ref=dst, send_sem=ss, recv_sem=rs, device_id=where, device_id_type=MESH
        )
        c.start()
        return c

    def got(ref, sem):
        pltpu.make_async_remote_copy(
            src_ref=ref, dst_ref=ref, send_sem=sem, recv_sem=sem, device_id=at_x, device_id_type=MESH
        ).wait_recv()

    locals_ = []
    for c in range(4):
        locals_.append(
            pltpu.make_async_copy(
                patches.at[:, pl.ds(c * wide, wide)], slabs.at[b, c, 0], sem_loc.at[c]
            )
        )
    locals_.append(pltpu.make_async_copy(cot, slabs.at[b, h, 1], sem_loc.at[4]))
    locals_.append(pltpu.make_async_copy(taps, tp, sem_loc.at[5]))
    locals_.append(pltpu.make_async_copy(mask_in, mask, sem_loc.at[6]))
    weights = [
        pltpu.make_async_copy(src, dst, sem_w.at[i])
        for i, (src, dst) in enumerate(((w_query, wq), (w_key, wk), (w_value, wv), (w_output, wo)))
    ]
    for c in locals_ + weights:
        c.start()
    barrier = pltpu.get_barrier_semaphore()
    for where in at_peer + [at_x, at_c, at_d]:
        pl.semaphore_signal(barrier, inc=1, device_id=where, device_id_type=MESH)
    pl.semaphore_wait(barrier, n + 2)

    sent = []
    own_cols = pl.ds(pl.multiple_of(h * wide, wide), wide)
    for k, where in enumerate(at_peer):
        sent.append(send(patches.at[:, own_cols], slabs.at[b, h, 0], zs.at[0, k], zr.at[0, b], where))
        sent.append(send(cot, slabs.at[b, h, 1], zs.at[1, k], zr.at[1, b], where))
    sent.append(send(cot, slabs.at[b, h, 1], xs.at[0], xr.at[b], at_x))
    sent.append(send(cot, slabs.at[b, h, 1], cs.at[0, 0], cr.at[0, b], at_c))
    for k, p in enumerate(peers):
        got(slabs.at[p, h, 0], zr.at[0, p])
        got(slabs.at[p, h, 1], zr.at[1, p])
        sent.append(send(slabs.at[p, h], slabs.at[p, h], xs.at[k + 1], xr.at[p], at_x))
        sent.append(send(slabs.at[p, h], slabs.at[p, h], cs.at[0, k + 1], cr.at[0, p], at_c))
    for c in locals_ + weights:
        c.wait()

    acc[...] = jnp.zeros_like(acc)
    row_of = lax.broadcasted_iota(jnp.int32, (n * rows, wide), 0)

    def quarter(c):
        cols = pl.ds(pl.multiple_of(c * wide, wide), wide)
        plain = slabs[:, c, 0].reshape(n * rows, wide).astype(F32)
        before = jnp.where(row_of == 0, 0.0, pltpu.roll(plain, 1, 0))
        after = jnp.where(row_of == n * rows - 1, 0.0, pltpu.roll(plain, n * rows - 1, 0))
        t = tp[:, cols]
        m = (plain + t[0:1] * before + t[1:2] * plain + t[2:3] * after).astype(BF)
        mixed[c] = m
        cq = slabs[:, c, 1].reshape(n * rows, wide)
        acc[0] += dot(m, wq[cols, :], 1, 0)
        acc[1] += dot(m, wk[cols, :], 1, 0)
        acc[2] += dot(m, wv[cols, :], 1, 0)
        acc[3] += dot(cq, wo[cols, :], 1, 0)

    quarter(h)
    got(slabs.at[b, hx, 1], xr.at[b])
    sent.append(send(slabs.at[b, hx, 1], slabs.at[b, hx, 1], cs.at[1, 0], cr.at[1, b], at_c))
    for k, p in enumerate(peers):
        got(slabs.at[p, hx], xr.at[p])
        sent.append(send(slabs.at[p, hx], slabs.at[p, hx], cs.at[1, k + 1], cr.at[1, p], at_c))
    quarter(hx)
    got(slabs.at[b, hc, 1], cr.at[0, b])
    for p in peers:
        got(slabs.at[p, hc], cr.at[0, p])
    quarter(hc)
    got(slabs.at[b, hd, 1], cr.at[1, b])
    for p in peers:
        got(slabs.at[p, hd], cr.at[1, p])
    quarter(hd)

    for i in range(4):
        heads4[i] = acc[i].astype(BF)

    for j in range(local):
        mine = slice(j * hs, (j + 1) * hs)
        keys, values = heads4[1, :, mine], heads4[2, :, mine]
        slot = j % 2
        for i in range(n):
            here = slice(i * rows, (i + 1) * rows)
            query, grad = heads4[0, here, mine], heads4[3, here, mine]
            allowed = (
                jnp.concatenate([jnp.full((rows, TILE), mask[i, t], jnp.int32) for t in range(n)], axis=1)
                == 1
            )
            score = dot(query, keys, 1, 1) * scale
            weight = jnp.where(allowed, jnp.exp(jnp.where(allowed, score, 0.0)), 0.0)
            inverse = 1.0 / jnp.sum(weight, -1, keepdims=True)
            att32 = dot(weight.astype(BF), values, 1, 0) * inverse
            delta = jnp.sum(grad.astype(F32) * att32, -1, keepdims=True)
            prob = weight * inverse
            dprob = dot(grad, values, 1, 1)
            dscore = (prob * (dprob - delta) * scale).astype(BF)
            probs[slot, here] = prob.astype(BF)
            dscores[slot, here] = dscore
            grads[here, 3 * wide + j * hs : 3 * wide + (j + 1) * hs] = att32.astype(BF)
            grads[here, mine] = dot(dscore, keys, 1, 0).astype(BF)
        grads[:, wide + j * hs : wide + (j + 1) * hs] = dot(
            dscores[slot], heads4[0, :, mine], 0, 0
        ).astype(BF)
        grads[:, 2 * wide + j * hs : 2 * wide + (j + 1) * hs] = dot(
            probs[slot], heads4[3, :, mine], 0, 0
        ).astype(BF)

    own_rows = pl.ds(pl.multiple_of(b * rows, rows), rows)
    grad_q = grads[own_rows, :wide]
    grad_k = grads[own_rows, wide : 2 * wide]
    grad_v = grads[own_rows, 2 * wide : 3 * wide]

    def branch(c):
        cols = pl.ds(pl.multiple_of(c * wide, wide), wide)
        return (
            dot(grad_q, wq[cols, :], 1, 1) + dot(grad_k, wk[cols, :], 1, 1)
            + dot(grad_v, wv[cols, :], 1, 1)
        )

    for k, (c, where) in enumerate(((hx, at_x), (hd, at_d), (hc, at_c))):
        part_out[k] = branch(c).astype(BF)
        sent.append(send(part_out.at[k], part_in.at[k], ps.at[k], pr.at[k], where))
    three = dot(mixed[b], grads[:, : 3 * wide], 0, 0) * norm
    for i in range(3):
        held[i] = three[:, i * wide : (i + 1) * wide]
    held[3] = dot(slabs[:, b, 1].reshape(n * rows, wide), grads[:, 3 * wide :], 0, 0) * norm
    writes = [
        pltpu.make_async_copy(held.at[i], out, sem_w.at[i])
        for i, out in enumerate((out_q, out_k, out_v, out_o))
    ]
    for c in writes:
        c.start()
    total = branch(h) + slabs[b, h, 1].astype(F32)
    for k in range(3):
        got(part_in.at[k], pr.at[k])
        total = total + part_in[k].astype(F32)

    first_row = lax.broadcasted_iota(jnp.int32, (rows, wide), 0) == 0
    last_row = lax.broadcasted_iota(jnp.int32, (rows, wide), 0) == rows - 1
    low, high = lax.rem(b + n - 1, n), lax.rem(b + 1, n)
    plain = slabs[b, h, 0].astype(F32)
    edge_low = jnp.where(b > 0, slabs[low, h, 0, rows - 16 :].astype(F32)[15:16], 0.0)
    edge_high = jnp.where(b < n - 1, slabs[high, h, 0, :16].astype(F32)[0:1], 0.0)
    before = jnp.where(first_row, edge_low, pltpu.roll(plain, 1, 0))
    after = jnp.where(last_row, edge_high, pltpu.roll(plain, rows - 1, 0))
    edge_out[0:1] = jnp.sum(total * before, 0, keepdims=True)
    edge_out[1:2] = jnp.sum(total * plain, 0, keepdims=True)
    edge_out[2:3] = jnp.sum(total * after, 0, keepdims=True)
    edge_out[3:4] = total[0:1]
    edge_out[4:5] = total[rows - 1 :]
    edge_out[5:8] = jnp.zeros((3, wide), F32)
    for k, where in enumerate(at_peer):
        sent.append(send(edge_out, edge_in.at[b], es.at[k], er.at[b], where))
    edge_in[b] = edge_out[...]

    for p in peers:
        got(edge_in.at[p], er.at[p])
    summed = edge_in[0]
    for j in range(1, n):
        summed = summed + edge_in[j]
    out_conv[...] = summed[0:3] * norm
    t = tp[:, own_cols]
    edge_low = jnp.where(b > 0, edge_in[low][4:5], 0.0)
    edge_high = jnp.where(b < n - 1, edge_in[high][3:4], 0.0)
    before = jnp.where(first_row, edge_low, pltpu.roll(total, 1, 0))
    after = jnp.where(last_row, edge_high, pltpu.roll(total, rows - 1, 0))
    out_in[...] = total * (1.0 + t[1:2]) + t[0:1] * after + t[2:3] * before
    for c in sent:
        c.wait_send()
    for c in writes:
        c.wait()


def placed(*refs):
    ins, outs, held, sems = refs[:6], refs[6:12], refs[12:18], refs[18]
    loads = [pltpu.make_async_copy(ins[i], held[i], sems.at[0, i]) for i in range(6)]
    stores = [pltpu.make_async_copy(held[i], outs[i], sems.at[1, i]) for i in range(6)]
    for c in loads:
        c.start()
    for load, store in zip(loads, stores):
        load.wait()
        store.start()
    for c in stores:
        c.wait()


def fused_device(patches, conv_taps, w_query, w_key, w_value, w_output, tile_mask, cotangent):
    n = lax.axis_size("blk")
    rows, wide = cotangent.shape
    hs = D // HEADS
    tokens = n * rows
    dma = pltpu.SemaphoreType.DMA
    anywhere = pl.BlockSpec(memory_space=pltpu.HBM)
    vmem = pl.BlockSpec(memory_space=pltpu.VMEM)
    square = jax.ShapeDtypeStruct((D // n, wide), F32)
    shapes = (
        jax.ShapeDtypeStruct((rows, wide), F32),
        jax.ShapeDtypeStruct((3, wide), F32),
    ) + (square,) * 4
    results = pl.pallas_call(
        functools.partial(fused, n, tokens ** (-0.5)),
        out_shape=shapes,
        in_specs=[anywhere] * 8,
        out_specs=(vmem, vmem) + (anywhere,) * 4,
        scratch_shapes=[
            pltpu.SMEM((n, n), jnp.int32),
            pltpu.VMEM((n, 4, 2, rows, wide), BF),
            pltpu.VMEM((4, tokens, wide), BF),
            pltpu.VMEM((D, wide), BF),
            pltpu.VMEM((D, wide), BF),
            pltpu.VMEM((D, wide), BF),
            pltpu.VMEM((D, wide), BF),
            pltpu.VMEM((3, D), F32),
            pltpu.VMEM((4, tokens, wide), F32),
            pltpu.VMEM((4, tokens, wide), BF),
            pltpu.VMEM((tokens, 4 * wide), BF),
            pltpu.VMEM((2, tokens, tokens), BF),
            pltpu.VMEM((2, tokens, tokens), BF),
            pltpu.VMEM((4, D // n, wide), F32),
            pltpu.VMEM((3, rows, wide), BF),
            pltpu.VMEM((3, rows, wide), BF),
            pltpu.VMEM((8, wide), F32),
            pltpu.VMEM((n, 8, wide), F32),
            dma((8,)), dma((4,)),
            dma((2, n - 1)), dma((2, n)),
            dma((n,)), dma((n,)),
            dma((2, n)), dma((2, n)),
            dma((3,)), dma((3,)),
            dma((n - 1,)), dma((n,)),
        ],
        compiler_params=pltpu.CompilerParams(
            collective_id=0, has_side_effects=True, vmem_limit_bytes=60 * 1024 * 1024
        ),
    )(patches, conv_taps, w_query, w_key, w_value, w_output, tile_mask, cotangent)
    return pl.pallas_call(
        placed,
        out_shape=shapes,
        in_specs=[anywhere] * 6,
        out_specs=(anywhere,) * 6,
        scratch_shapes=[pltpu.VMEM(t.shape, F32) for t in shapes] + [dma((2, 6))],
        compiler_params=pltpu.CompilerParams(vmem_limit_bytes=60 * 1024 * 1024),
    )(*results)


def fits(mesh):
    shape = mesh.shape
    n = shape["blk"]
    return n == 4 and shape["heads"] == 2 and shape["sub"] == 2 and HEADS == 4 * n


def solution(mesh):
    in_specs = (
        P(("groups", "blk"), None),
        P(),
        P(None, ("heads", "sub")),
        P(None, ("heads", "sub")),
        P(None, ("heads", "sub")),
        P(None, ("heads", "sub")),
        P("groups", None),
        P(("groups", "blk"), ("heads", "sub")),
    )
    out_specs = (
        P(("groups", "blk"), ("heads", "sub")),
        P("groups", ("heads", "sub")),
        P(("groups", "blk"), ("heads", "sub")),
        P(("groups", "blk"), ("heads", "sub")),
        P(("groups", "blk"), ("heads", "sub")),
        P(("groups", "blk"), ("heads", "sub")),
    )
    return jax.shard_map(
        fused_device if fits(mesh) else per_device, mesh=mesh, in_specs=in_specs, out_specs=out_specs, check_vma=False
    )
```

```python
import functools

import jax
import jax.numpy as jnp
from jax import lax
from jax.experimental import pallas as pl
from jax.experimental.pallas import tpu as pltpu
from jax.sharding import PartitionSpec as P

D = 1024
HEADS = 16
TILE = 128


def padded(cells, sides, width):
    for axis, dim in sides:
        count = lax.axis_size(axis)
        ends = count - 1
        head = lax.slice_in_dim(cells, 0, width, axis=dim)
        tail = lax.slice_in_dim(cells, cells.shape[dim] - width, cells.shape[dim], axis=dim)
        cells = jnp.concatenate(
            [
                lax.ppermute(tail, axis, [(i, (i + 1) % count) for i in range(ends)]),
                cells,
                lax.ppermute(head, axis, [((i + 1) % count, i) for i in range(ends)]),
            ],
            axis=dim,
        )
    return cells


def from_behind(value, axis, steps):
    count = lax.axis_size(axis)
    pairs = [(source, (source + steps) % count) for source in range(count)]
    return lax.ppermute(value, axis, pairs)


def allowed_rows(mask_bf, first_query, query_count, first_key, key_count):
    tiles = mask_bf.shape[0]
    columns = jnp.arange(tiles, dtype=jnp.int32)
    query_tiles = (first_query + jnp.arange(query_count, dtype=jnp.int32)) // TILE
    key_tiles = (first_key + jnp.arange(key_count, dtype=jnp.int32)) // TILE
    query_hot = (query_tiles[:, None] == columns[None, :]).astype(jnp.bfloat16)
    key_hot = (key_tiles[:, None] == columns[None, :]).astype(jnp.bfloat16)
    picked = jnp.dot(query_hot, mask_bf, preferred_element_type=jnp.float32).astype(jnp.bfloat16)
    return jnp.einsum("qn,kn->qk", picked, key_hot, preferred_element_type=jnp.float32) > 0.5


def per_device(patches, conv_taps, w_query, w_key, w_value, w_output, tile_mask, cotangent):
    rows = patches.shape[0]
    local = w_query.shape[1]
    head_size = D // HEADS
    heads_here = local // head_size
    cycle_size = lax.axis_size("blk")
    position = lax.axis_index("blk")
    total_rows = rows * cycle_size
    scale = head_size ** (-0.5)
    norm = total_rows ** (-0.5)
    mask_bf = tile_mask.astype(jnp.bfloat16)
    first_query = position * rows
    padded_in = padded(patches, (("blk", 0),), 1)
    padded32 = padded_in.astype(jnp.float32)
    middle = padded32[1:-1]
    mixed = (
        middle + conv_taps[0] * padded32[:-2] + conv_taps[1] * middle + conv_taps[2] * padded32[2:]
    ).astype(jnp.bfloat16)
    queries = jnp.dot(mixed, w_query, preferred_element_type=jnp.float32).astype(jnp.bfloat16)
    keys_own = jnp.dot(mixed, w_key, preferred_element_type=jnp.float32).astype(jnp.bfloat16)
    values_own = jnp.dot(mixed, w_value, preferred_element_type=jnp.float32).astype(jnp.bfloat16)
    keys_all, values_all = (
        lax.all_gather(keys_own, "blk", axis=0, tiled=True),
        lax.all_gather(values_own, "blk", axis=0, tiled=True),
    )
    cot_full = lax.all_gather(cotangent, ("heads", "sub"), axis=1, tiled=True)
    grad_att = jnp.dot(cot_full, w_output, preferred_element_type=jnp.float32).astype(jnp.bfloat16)
    group = 1
    for power in range(12):
        if group * 2 * rows <= 1024 and cycle_size % (group * 2) == 0:
            group = group * 2
    span = group * rows
    blocks = cycle_size // group
    query_heads = queries.reshape(rows, heads_here, head_size)
    grad_heads = grad_att.reshape(rows, heads_here, head_size)
    key_blocks = keys_all.reshape(blocks, span, heads_here, head_size)
    value_blocks = values_all.reshape(blocks, span, heads_here, head_size)
    block_ids = jnp.arange(blocks, dtype=jnp.int32)

    def weights_of(key_block, allowed):
        raw = (
            jnp.einsum("qhd,khd->hqk", query_heads, key_block, preferred_element_type=jnp.float32)
            * scale
        )
        return jnp.where(allowed[None], jnp.exp(jnp.where(allowed[None], raw, 0.0)), 0.0)

    def forward_step(state, inputs):
        block_id, key_block, value_block = inputs
        allowed = allowed_rows(mask_bf, first_query, rows, block_id * span, span)
        accum, totals = state
        weights = weights_of(key_block, allowed)
        added = jnp.einsum(
            "hqk,khd->hqd",
            weights.astype(jnp.bfloat16),
            value_block,
            preferred_element_type=jnp.float32,
        )
        state = (accum + added, totals + jnp.sum(weights, -1))
        return (state, None)

    start_state = (
        jnp.zeros((heads_here, rows, head_size), jnp.float32),
        jnp.zeros((heads_here, rows), jnp.float32),
    )
    (accum, totals), unused = lax.scan(
        forward_step, start_state, (block_ids, key_blocks, value_blocks)
    )
    attended32 = accum / totals[:, :, None]
    attended = jnp.transpose(attended32, (1, 0, 2)).reshape(rows, local).astype(jnp.bfloat16)
    deltas = jnp.einsum("qhd,hqd->hq", grad_heads.astype(jnp.float32), attended32)

    def local_grads(key_block, value_block, allowed):
        weights = weights_of(key_block, allowed)
        probs = weights / totals[:, :, None]
        dprobs = jnp.einsum(
            "qhd,khd->hqk", grad_heads, value_block, preferred_element_type=jnp.float32
        )
        dscores = (probs * (dprobs - deltas[:, :, None]) * scale).astype(jnp.bfloat16)
        return (
            jnp.einsum("hqk,khd->qhd", dscores, key_block, preferred_element_type=jnp.float32),
            jnp.einsum("hqk,qhd->khd", dscores, query_heads, preferred_element_type=jnp.float32),
            jnp.einsum(
                "hqk,qhd->khd",
                probs.astype(jnp.bfloat16),
                grad_heads,
                preferred_element_type=jnp.float32,
            ),
        )

    def shard_grads(block):
        wrapped = jnp.remainder(block, cycle_size)
        key_block = lax.dynamic_slice_in_dim(keys_all, wrapped * rows, rows, 0).reshape(
            rows, heads_here, head_size
        )
        value_block = lax.dynamic_slice_in_dim(values_all, wrapped * rows, rows, 0).reshape(
            rows, heads_here, head_size
        )
        allowed = allowed_rows(mask_bf, first_query, rows, wrapped * rows, rows)
        query_add, key_term, value_term = local_grads(key_block, value_block, allowed)
        return (
            query_add,
            jnp.stack([key_term.reshape(rows, local), value_term.reshape(rows, local)]),
        )

    query_first, carried_first = shard_grads(position - 1)

    def turn(step, state):
        accum_q, carried = state
        moved = from_behind(carried, "blk", 1)
        query_add, term = shard_grads(position - step - 1)
        return (accum_q + query_add, moved + term)

    accum_q, summed = lax.fori_loop(1, cycle_size, turn, (query_first, carried_first))
    grad_keys = summed[0].astype(jnp.bfloat16)
    grad_values = summed[1].astype(jnp.bfloat16)
    grad_queries = accum_q.reshape(rows, local).astype(jnp.bfloat16)
    stacked = jnp.stack(
        [
            jnp.einsum("td,tc->dc", mixed, grad_queries, preferred_element_type=jnp.float32),
            jnp.einsum("td,tc->dc", mixed, grad_keys, preferred_element_type=jnp.float32),
            jnp.einsum("td,tc->dc", mixed, grad_values, preferred_element_type=jnp.float32),
            jnp.einsum("td,tc->dc", cot_full, attended, preferred_element_type=jnp.float32),
        ]
    )
    weight_sums = lax.psum_scatter(stacked, "blk", scatter_dimension=1, tiled=True) * norm
    partial_grad = (
        jnp.einsum("tc,dc->td", grad_queries, w_query, preferred_element_type=jnp.float32)
        + jnp.einsum("tc,dc->td", grad_keys, w_key, preferred_element_type=jnp.float32)
        + jnp.einsum("tc,dc->td", grad_values, w_value, preferred_element_type=jnp.float32)
    )
    grad_mixed = lax.psum_scatter(
        partial_grad, ("heads", "sub"), scatter_dimension=1, tiled=True
    ) + cotangent.astype(jnp.float32)
    columns_here = cotangent.shape[1]
    offset = lax.axis_index(("heads", "sub")) * columns_here
    taps_here = lax.dynamic_slice_in_dim(conv_taps, offset, columns_here, 1)
    padded_grad = padded(grad_mixed.astype(jnp.bfloat16), (("blk", 0),), 1).astype(grad_mixed.dtype)
    input_grad = (
        grad_mixed * (1.0 + taps_here[1])
        + taps_here[0] * padded_grad[2:]
        + taps_here[2] * padded_grad[:-2]
    )
    patch_cols = lax.dynamic_slice_in_dim(padded32, offset, columns_here, 1)
    conv_terms = jnp.stack(
        [
            jnp.sum(grad_mixed * patch_cols[:-2], 0),
            jnp.sum(grad_mixed * patch_cols[1:-1], 0),
            jnp.sum(grad_mixed * patch_cols[2:], 0),
        ]
    )
    conv_grad = lax.psum(conv_terms, "blk") * norm
    return (input_grad, conv_grad, weight_sums[0], weight_sums[1], weight_sums[2], weight_sums[3])

MESH = pl.DeviceIdType.MESH
BF = jnp.bfloat16
F32 = jnp.float32


def dot(a, b, ca, cb):
    return lax.dot_general(a, b, (((ca,), (cb,)), ((), ())), preferred_element_type=F32)


def fused(
    n, norm,
    patches, taps, w_query, w_key, w_value, w_output, mask_in, cot,
    out_in, out_conv, out_q, out_k, out_v, out_o,
    mask, slabs, mixed, wq, wk, wv, wo, tp, acc, heads4, grads, probs, dscores, held,
    part_out, part_in, edge_out, edge_in,
    sem_loc, sem_w, zs, zr, xs, xr, cs, cr, ps, pr, es, er,
):
    g = lax.axis_index("groups")
    b = lax.axis_index("blk")
    x = lax.axis_index("heads")
    s = lax.axis_index("sub")
    h, hx, hc, hd = x * 2 + s, (1 - x) * 2 + s, x * 2 + 1 - s, (1 - x) * 2 + 1 - s
    rows = patches.shape[0]
    wide = cot.shape[1]
    local = wide // (D // HEADS)
    hs = D // HEADS
    scale = hs ** (-0.5)
    peers = [lax.rem(b + k, n) for k in range(1, n)]
    at_peer = [(g, p, x, s) for p in peers]
    at_x, at_c, at_d = (g, b, 1 - x, s), (g, b, x, 1 - s), (g, b, 1 - x, 1 - s)

    def send(src, dst, ss, rs, where):
        c = pltpu.make_async_remote_copy(
            src_ref=src, dst_ref=dst, send_sem=ss, recv_sem=rs, device_id=where, device_id_type=MESH
        )
        c.start()
        return c

    def got(ref, sem):
        pltpu.make_async_remote_copy(
            src_ref=ref, dst_ref=ref, send_sem=sem, recv_sem=sem, device_id=at_x, device_id_type=MESH
        ).wait_recv()

    locals_ = []
    for c in range(4):
        locals_.append(
            pltpu.make_async_copy(
                patches.at[:, pl.ds(c * wide, wide)], slabs.at[b, c, 0], sem_loc.at[c]
            )
        )
    locals_.append(pltpu.make_async_copy(cot, slabs.at[b, h, 1], sem_loc.at[4]))
    locals_.append(pltpu.make_async_copy(taps, tp, sem_loc.at[5]))
    locals_.append(pltpu.make_async_copy(mask_in, mask, sem_loc.at[6]))
    weights = [
        pltpu.make_async_copy(src, dst, sem_w.at[i])
        for i, (src, dst) in enumerate(((w_query, wq), (w_key, wk), (w_value, wv), (w_output, wo)))
    ]
    for c in locals_ + weights:
        c.start()
    barrier = pltpu.get_barrier_semaphore()
    for where in at_peer + [at_x, at_c, at_d]:
        pl.semaphore_signal(barrier, inc=1, device_id=where, device_id_type=MESH)
    pl.semaphore_wait(barrier, n + 2)

    sent, relays = [], []
    own_cols = pl.ds(pl.multiple_of(h * wide, wide), wide)
    middle = lax.rem((b + 1) // 2, 2)
    inner, outer, across = b + 1 - 2 * (b // 2), middle * 3 * (b - 1), lax.rem(b + 2, n)
    last = 3 * (1 - lax.rem(b, 2))
    order = [
        inner,
        middle * last + (1 - middle) * across,
        middle * across + (1 - middle) * last,
    ]
    own_parts = (patches.at[:, own_cols], cot)

    def relay(src, t, kind, k, where):
        c = pltpu.make_async_remote_copy(
            src_ref=src, dst_ref=slabs.at[t, h, kind], send_sem=zs.at[kind, k],
            recv_sem=zr.at[kind, t], device_id=where, device_id_type=MESH,
        )
        pl.when(middle == 1)(c.start)
        relays.append(c)

    at_inner, at_outer = (g, inner, x, s), (g, outer, x, s)
    for kind in (1, 0):
        sent.append(
            send(own_parts[kind], slabs.at[b, h, kind], zs.at[kind, 0], zr.at[kind, b], at_inner)
        )
        relay(own_parts[kind], b, kind, 1, at_outer)
        if kind == 1:
            sent.append(send(cot, slabs.at[b, h, 1], xs.at[1, 0], xr.at[1, b], at_x))
            sent.append(send(cot, slabs.at[b, h, 1], cs.at[0, 1, 0], cr.at[0, 1, b], at_c))

    def from_z(k):
        p = order[k]
        for kind in (1, 0):
            part = slabs.at[p, h, kind]
            got(part, zr.at[kind, p])
            relay(part, p, kind, k + 2, at_inner if k == 1 else at_outer)
            sent.append(send(part, part, xs.at[kind, k + 1], xr.at[kind, p], at_x))
            sent.append(send(part, part, cs.at[0, kind, k + 1], cr.at[0, kind, p], at_c))

    def from_x(k):
        p = order[k] if k >= 0 else b
        for kind in (1, 0) if k >= 0 else (1,):
            part = slabs.at[p, hx, kind]
            got(part, xr.at[kind, p])
            sent.append(send(part, part, cs.at[1, kind, k + 1], cr.at[1, kind, p], at_c))

    def from_core(i, c):
        got(slabs.at[b, c, 1], cr.at[i, 1, b])
        for p in order:
            for kind in (1, 0):
                got(slabs.at[p, c, kind], cr.at[i, kind, p])

    from_z(0)
    from_x(-1)
    from_z(1)
    from_x(0)
    from_z(2)
    for c in locals_ + weights:
        c.wait()

    acc[...] = jnp.zeros_like(acc)
    row_of = lax.broadcasted_iota(jnp.int32, (n * rows, wide), 0)

    def quarter(c):
        cols = pl.ds(pl.multiple_of(c * wide, wide), wide)
        plain = slabs[:, c, 0].reshape(n * rows, wide).astype(F32)
        before = jnp.where(row_of == 0, 0.0, pltpu.roll(plain, 1, 0))
        after = jnp.where(row_of == n * rows - 1, 0.0, pltpu.roll(plain, n * rows - 1, 0))
        t = tp[:, cols]
        m = (plain + t[0:1] * before + t[1:2] * plain + t[2:3] * after).astype(BF)
        mixed[c] = m
        cq = slabs[:, c, 1].reshape(n * rows, wide)
        acc[0] += dot(m, wq[cols, :], 1, 0)
        acc[1] += dot(m, wk[cols, :], 1, 0)
        acc[2] += dot(m, wv[cols, :], 1, 0)
        acc[3] += dot(cq, wo[cols, :], 1, 0)

    quarter(h)
    from_x(1)
    from_x(2)
    from_core(0, hc)
    quarter(hc)
    quarter(hx)
    from_core(1, hd)
    quarter(hd)

    for i in range(4):
        heads4[i] = acc[i].astype(BF)

    for j in range(local):
        mine = slice(j * hs, (j + 1) * hs)
        keys, values = heads4[1, :, mine], heads4[2, :, mine]
        slot = j % 2
        for i in range(n):
            here = slice(i * rows, (i + 1) * rows)
            query, grad = heads4[0, here, mine], heads4[3, here, mine]
            allowed = (
                jnp.concatenate([jnp.full((rows, TILE), mask[i, t], jnp.int32) for t in range(n)], axis=1)
                == 1
            )
            score = dot(query, keys, 1, 1) * scale
            weight = jnp.where(allowed, jnp.exp(jnp.where(allowed, score, 0.0)), 0.0)
            inverse = 1.0 / jnp.sum(weight, -1, keepdims=True)
            att32 = dot(weight.astype(BF), values, 1, 0) * inverse
            delta = jnp.sum(grad.astype(F32) * att32, -1, keepdims=True)
            prob = weight * inverse
            dprob = dot(grad, values, 1, 1)
            dscore = (prob * (dprob - delta) * scale).astype(BF)
            probs[slot, here] = prob.astype(BF)
            dscores[slot, here] = dscore
            grads[here, 3 * wide + j * hs : 3 * wide + (j + 1) * hs] = att32.astype(BF)
            grads[here, mine] = dot(dscore, keys, 1, 0).astype(BF)
        grads[:, wide + j * hs : wide + (j + 1) * hs] = dot(
            dscores[slot], heads4[0, :, mine], 0, 0
        ).astype(BF)
        grads[:, 2 * wide + j * hs : 2 * wide + (j + 1) * hs] = dot(
            probs[slot], heads4[3, :, mine], 0, 0
        ).astype(BF)

    own_rows = pl.ds(pl.multiple_of(b * rows, rows), rows)
    grad_q = grads[own_rows, :wide]
    grad_k = grads[own_rows, wide : 2 * wide]
    grad_v = grads[own_rows, 2 * wide : 3 * wide]

    def branch(c):
        cols = pl.ds(pl.multiple_of(c * wide, wide), wide)
        return (
            dot(grad_q, wq[cols, :], 1, 1) + dot(grad_k, wk[cols, :], 1, 1)
            + dot(grad_v, wv[cols, :], 1, 1)
        )

    for k, (c, where) in enumerate(((hx, at_x), (hd, at_d), (hc, at_c))):
        part_out[k] = branch(c).astype(BF)
        sent.append(send(part_out.at[k], part_in.at[k], ps.at[k], pr.at[k], where))
    three = dot(mixed[b], grads[:, : 3 * wide], 0, 0) * norm
    for i in range(3):
        held[i] = three[:, i * wide : (i + 1) * wide]
    held[3] = dot(slabs[:, b, 1].reshape(n * rows, wide), grads[:, 3 * wide :], 0, 0) * norm
    writes = [
        pltpu.make_async_copy(held.at[i], out, sem_w.at[i])
        for i, out in enumerate((out_q, out_k, out_v, out_o))
    ]
    for c in writes:
        c.start()
    total = branch(h) + slabs[b, h, 1].astype(F32)
    for k in range(3):
        got(part_in.at[k], pr.at[k])
        total = total + part_in[k].astype(F32)

    first_row = lax.broadcasted_iota(jnp.int32, (rows, wide), 0) == 0
    last_row = lax.broadcasted_iota(jnp.int32, (rows, wide), 0) == rows - 1
    low, high = lax.rem(b + n - 1, n), lax.rem(b + 1, n)
    plain = slabs[b, h, 0].astype(F32)
    edge_low = jnp.where(b > 0, slabs[low, h, 0, rows - 16 :].astype(F32)[15:16], 0.0)
    edge_high = jnp.where(b < n - 1, slabs[high, h, 0, :16].astype(F32)[0:1], 0.0)
    before = jnp.where(first_row, edge_low, pltpu.roll(plain, 1, 0))
    after = jnp.where(last_row, edge_high, pltpu.roll(plain, rows - 1, 0))
    edge_out[0:1] = jnp.sum(total * before, 0, keepdims=True)
    edge_out[1:2] = jnp.sum(total * plain, 0, keepdims=True)
    edge_out[2:3] = jnp.sum(total * after, 0, keepdims=True)
    edge_out[3:4] = total[0:1]
    edge_out[4:5] = total[rows - 1 :]
    edge_out[5:8] = jnp.zeros((3, wide), F32)
    for k, where in enumerate(at_peer):
        sent.append(send(edge_out, edge_in.at[b], es.at[k], er.at[b], where))
    edge_in[b] = edge_out[...]

    for p in peers:
        got(edge_in.at[p], er.at[p])
    summed = edge_in[0]
    for j in range(1, n):
        summed = summed + edge_in[j]
    out_conv[...] = summed[0:3] * norm
    t = tp[:, own_cols]
    edge_low = jnp.where(b > 0, edge_in[low][4:5], 0.0)
    edge_high = jnp.where(b < n - 1, edge_in[high][3:4], 0.0)
    before = jnp.where(first_row, edge_low, pltpu.roll(total, 1, 0))
    after = jnp.where(last_row, edge_high, pltpu.roll(total, rows - 1, 0))
    out_in[...] = total * (1.0 + t[1:2]) + t[0:1] * after + t[2:3] * before
    for c in sent:
        c.wait_send()
    for c in relays:
        pl.when(middle == 1)(c.wait_send)
    for c in writes:
        c.wait()


def placed(*refs):
    ins, outs, held, sems = refs[:6], refs[6:12], refs[12:18], refs[18]
    loads = [pltpu.make_async_copy(ins[i], held[i], sems.at[0, i]) for i in range(6)]
    stores = [pltpu.make_async_copy(held[i], outs[i], sems.at[1, i]) for i in range(6)]
    for c in loads:
        c.start()
    for load, store in zip(loads, stores):
        load.wait()
        store.start()
    for c in stores:
        c.wait()


def fused_device(patches, conv_taps, w_query, w_key, w_value, w_output, tile_mask, cotangent):
    n = lax.axis_size("blk")
    rows, wide = cotangent.shape
    hs = D // HEADS
    tokens = n * rows
    dma = pltpu.SemaphoreType.DMA
    anywhere = pl.BlockSpec(memory_space=pltpu.HBM)
    vmem = pl.BlockSpec(memory_space=pltpu.VMEM)
    square = jax.ShapeDtypeStruct((D // n, wide), F32)
    shapes = (
        jax.ShapeDtypeStruct((rows, wide), F32),
        jax.ShapeDtypeStruct((3, wide), F32),
    ) + (square,) * 4
    results = pl.pallas_call(
        functools.partial(fused, n, tokens ** (-0.5)),
        out_shape=shapes,
        in_specs=[anywhere] * 8,
        out_specs=(vmem, vmem) + (anywhere,) * 4,
        scratch_shapes=[
            pltpu.SMEM((n, n), jnp.int32),
            pltpu.VMEM((n, 4, 2, rows, wide), BF),
            pltpu.VMEM((4, tokens, wide), BF),
            pltpu.VMEM((D, wide), BF),
            pltpu.VMEM((D, wide), BF),
            pltpu.VMEM((D, wide), BF),
            pltpu.VMEM((D, wide), BF),
            pltpu.VMEM((3, D), F32),
            pltpu.VMEM((4, tokens, wide), F32),
            pltpu.VMEM((4, tokens, wide), BF),
            pltpu.VMEM((tokens, 4 * wide), BF),
            pltpu.VMEM((2, tokens, tokens), BF),
            pltpu.VMEM((2, tokens, tokens), BF),
            pltpu.VMEM((4, D // n, wide), F32),
            pltpu.VMEM((3, rows, wide), BF),
            pltpu.VMEM((3, rows, wide), BF),
            pltpu.VMEM((8, wide), F32),
            pltpu.VMEM((n, 8, wide), F32),
            dma((8,)), dma((4,)),
            dma((2, n + 1)), dma((2, n)),
            dma((2, n)), dma((2, n)),
            dma((2, 2, n)), dma((2, 2, n)),
            dma((3,)), dma((3,)),
            dma((n - 1,)), dma((n,)),
        ],
        compiler_params=pltpu.CompilerParams(
            collective_id=0, has_side_effects=True, vmem_limit_bytes=60 * 1024 * 1024
        ),
    )(patches, conv_taps, w_query, w_key, w_value, w_output, tile_mask, cotangent)
    return pl.pallas_call(
        placed,
        out_shape=shapes,
        in_specs=[anywhere] * 6,
        out_specs=(anywhere,) * 6,
        scratch_shapes=[pltpu.VMEM(t.shape, F32) for t in shapes] + [dma((2, 6))],
        compiler_params=pltpu.CompilerParams(vmem_limit_bytes=60 * 1024 * 1024),
    )(*results)


def fits(mesh):
    shape = mesh.shape
    n = shape["blk"]
    return n == 4 and shape["heads"] == 2 and shape["sub"] == 2 and HEADS == 4 * n


def solution(mesh):
    in_specs = (
        P(("groups", "blk"), None),
        P(),
        P(None, ("heads", "sub")),
        P(None, ("heads", "sub")),
        P(None, ("heads", "sub")),
        P(None, ("heads", "sub")),
        P("groups", None),
        P(("groups", "blk"), ("heads", "sub")),
    )
    out_specs = (
        P(("groups", "blk"), ("heads", "sub")),
        P("groups", ("heads", "sub")),
        P(("groups", "blk"), ("heads", "sub")),
        P(("groups", "blk"), ("heads", "sub")),
        P(("groups", "blk"), ("heads", "sub")),
        P(("groups", "blk"), ("heads", "sub")),
    )
    return jax.shard_map(
        fused_device if fits(mesh) else per_device, mesh=mesh, in_specs=in_specs, out_specs=out_specs, check_vma=False
    )
```

```python
import functools

import jax
import jax.numpy as jnp
from jax import lax
from jax.experimental import pallas as pl
from jax.experimental.pallas import tpu as pltpu
from jax.sharding import PartitionSpec as P

D = 1024
HEADS = 16
TILE = 128


def padded(cells, sides, width):
    for axis, dim in sides:
        count = lax.axis_size(axis)
        ends = count - 1
        head = lax.slice_in_dim(cells, 0, width, axis=dim)
        tail = lax.slice_in_dim(cells, cells.shape[dim] - width, cells.shape[dim], axis=dim)
        cells = jnp.concatenate(
            [
                lax.ppermute(tail, axis, [(i, (i + 1) % count) for i in range(ends)]),
                cells,
                lax.ppermute(head, axis, [((i + 1) % count, i) for i in range(ends)]),
            ],
            axis=dim,
        )
    return cells


def from_behind(value, axis, steps):
    count = lax.axis_size(axis)
    pairs = [(source, (source + steps) % count) for source in range(count)]
    return lax.ppermute(value, axis, pairs)


def allowed_rows(mask_bf, first_query, query_count, first_key, key_count):
    tiles = mask_bf.shape[0]
    columns = jnp.arange(tiles, dtype=jnp.int32)
    query_tiles = (first_query + jnp.arange(query_count, dtype=jnp.int32)) // TILE
    key_tiles = (first_key + jnp.arange(key_count, dtype=jnp.int32)) // TILE
    query_hot = (query_tiles[:, None] == columns[None, :]).astype(jnp.bfloat16)
    key_hot = (key_tiles[:, None] == columns[None, :]).astype(jnp.bfloat16)
    picked = jnp.dot(query_hot, mask_bf, preferred_element_type=jnp.float32).astype(jnp.bfloat16)
    return jnp.einsum("qn,kn->qk", picked, key_hot, preferred_element_type=jnp.float32) > 0.5


def per_device(patches, conv_taps, w_query, w_key, w_value, w_output, tile_mask, cotangent):
    rows = patches.shape[0]
    local = w_query.shape[1]
    head_size = D // HEADS
    heads_here = local // head_size
    cycle_size = lax.axis_size("blk")
    position = lax.axis_index("blk")
    total_rows = rows * cycle_size
    scale = head_size ** (-0.5)
    norm = total_rows ** (-0.5)
    mask_bf = tile_mask.astype(jnp.bfloat16)
    first_query = position * rows
    padded_in = padded(patches, (("blk", 0),), 1)
    padded32 = padded_in.astype(jnp.float32)
    middle = padded32[1:-1]
    mixed = (
        middle + conv_taps[0] * padded32[:-2] + conv_taps[1] * middle + conv_taps[2] * padded32[2:]
    ).astype(jnp.bfloat16)
    queries = jnp.dot(mixed, w_query, preferred_element_type=jnp.float32).astype(jnp.bfloat16)
    keys_own = jnp.dot(mixed, w_key, preferred_element_type=jnp.float32).astype(jnp.bfloat16)
    values_own = jnp.dot(mixed, w_value, preferred_element_type=jnp.float32).astype(jnp.bfloat16)
    keys_all, values_all = (
        lax.all_gather(keys_own, "blk", axis=0, tiled=True),
        lax.all_gather(values_own, "blk", axis=0, tiled=True),
    )
    cot_full = lax.all_gather(cotangent, ("heads", "sub"), axis=1, tiled=True)
    grad_att = jnp.dot(cot_full, w_output, preferred_element_type=jnp.float32).astype(jnp.bfloat16)
    group = 1
    for power in range(12):
        if group * 2 * rows <= 1024 and cycle_size % (group * 2) == 0:
            group = group * 2
    span = group * rows
    blocks = cycle_size // group
    query_heads = queries.reshape(rows, heads_here, head_size)
    grad_heads = grad_att.reshape(rows, heads_here, head_size)
    key_blocks = keys_all.reshape(blocks, span, heads_here, head_size)
    value_blocks = values_all.reshape(blocks, span, heads_here, head_size)
    block_ids = jnp.arange(blocks, dtype=jnp.int32)

    def weights_of(key_block, allowed):
        raw = (
            jnp.einsum("qhd,khd->hqk", query_heads, key_block, preferred_element_type=jnp.float32)
            * scale
        )
        return jnp.where(allowed[None], jnp.exp(jnp.where(allowed[None], raw, 0.0)), 0.0)

    def forward_step(state, inputs):
        block_id, key_block, value_block = inputs
        allowed = allowed_rows(mask_bf, first_query, rows, block_id * span, span)
        accum, totals = state
        weights = weights_of(key_block, allowed)
        added = jnp.einsum(
            "hqk,khd->hqd",
            weights.astype(jnp.bfloat16),
            value_block,
            preferred_element_type=jnp.float32,
        )
        state = (accum + added, totals + jnp.sum(weights, -1))
        return (state, None)

    start_state = (
        jnp.zeros((heads_here, rows, head_size), jnp.float32),
        jnp.zeros((heads_here, rows), jnp.float32),
    )
    (accum, totals), unused = lax.scan(
        forward_step, start_state, (block_ids, key_blocks, value_blocks)
    )
    attended32 = accum / totals[:, :, None]
    attended = jnp.transpose(attended32, (1, 0, 2)).reshape(rows, local).astype(jnp.bfloat16)
    deltas = jnp.einsum("qhd,hqd->hq", grad_heads.astype(jnp.float32), attended32)

    def local_grads(key_block, value_block, allowed):
        weights = weights_of(key_block, allowed)
        probs = weights / totals[:, :, None]
        dprobs = jnp.einsum(
            "qhd,khd->hqk", grad_heads, value_block, preferred_element_type=jnp.float32
        )
        dscores = (probs * (dprobs - deltas[:, :, None]) * scale).astype(jnp.bfloat16)
        return (
            jnp.einsum("hqk,khd->qhd", dscores, key_block, preferred_element_type=jnp.float32),
            jnp.einsum("hqk,qhd->khd", dscores, query_heads, preferred_element_type=jnp.float32),
            jnp.einsum(
                "hqk,qhd->khd",
                probs.astype(jnp.bfloat16),
                grad_heads,
                preferred_element_type=jnp.float32,
            ),
        )

    def shard_grads(block):
        wrapped = jnp.remainder(block, cycle_size)
        key_block = lax.dynamic_slice_in_dim(keys_all, wrapped * rows, rows, 0).reshape(
            rows, heads_here, head_size
        )
        value_block = lax.dynamic_slice_in_dim(values_all, wrapped * rows, rows, 0).reshape(
            rows, heads_here, head_size
        )
        allowed = allowed_rows(mask_bf, first_query, rows, wrapped * rows, rows)
        query_add, key_term, value_term = local_grads(key_block, value_block, allowed)
        return (
            query_add,
            jnp.stack([key_term.reshape(rows, local), value_term.reshape(rows, local)]),
        )

    query_first, carried_first = shard_grads(position - 1)

    def turn(step, state):
        accum_q, carried = state
        moved = from_behind(carried, "blk", 1)
        query_add, term = shard_grads(position - step - 1)
        return (accum_q + query_add, moved + term)

    accum_q, summed = lax.fori_loop(1, cycle_size, turn, (query_first, carried_first))
    grad_keys = summed[0].astype(jnp.bfloat16)
    grad_values = summed[1].astype(jnp.bfloat16)
    grad_queries = accum_q.reshape(rows, local).astype(jnp.bfloat16)
    stacked = jnp.stack(
        [
            jnp.einsum("td,tc->dc", mixed, grad_queries, preferred_element_type=jnp.float32),
            jnp.einsum("td,tc->dc", mixed, grad_keys, preferred_element_type=jnp.float32),
            jnp.einsum("td,tc->dc", mixed, grad_values, preferred_element_type=jnp.float32),
            jnp.einsum("td,tc->dc", cot_full, attended, preferred_element_type=jnp.float32),
        ]
    )
    weight_sums = lax.psum_scatter(stacked, "blk", scatter_dimension=1, tiled=True) * norm
    partial_grad = (
        jnp.einsum("tc,dc->td", grad_queries, w_query, preferred_element_type=jnp.float32)
        + jnp.einsum("tc,dc->td", grad_keys, w_key, preferred_element_type=jnp.float32)
        + jnp.einsum("tc,dc->td", grad_values, w_value, preferred_element_type=jnp.float32)
    )
    grad_mixed = lax.psum_scatter(
        partial_grad, ("heads", "sub"), scatter_dimension=1, tiled=True
    ) + cotangent.astype(jnp.float32)
    columns_here = cotangent.shape[1]
    offset = lax.axis_index(("heads", "sub")) * columns_here
    taps_here = lax.dynamic_slice_in_dim(conv_taps, offset, columns_here, 1)
    padded_grad = padded(grad_mixed.astype(jnp.bfloat16), (("blk", 0),), 1).astype(grad_mixed.dtype)
    input_grad = (
        grad_mixed * (1.0 + taps_here[1])
        + taps_here[0] * padded_grad[2:]
        + taps_here[2] * padded_grad[:-2]
    )
    patch_cols = lax.dynamic_slice_in_dim(padded32, offset, columns_here, 1)
    conv_terms = jnp.stack(
        [
            jnp.sum(grad_mixed * patch_cols[:-2], 0),
            jnp.sum(grad_mixed * patch_cols[1:-1], 0),
            jnp.sum(grad_mixed * patch_cols[2:], 0),
        ]
    )
    conv_grad = lax.psum(conv_terms, "blk") * norm
    return (input_grad, conv_grad, weight_sums[0], weight_sums[1], weight_sums[2], weight_sums[3])

MESH = pl.DeviceIdType.MESH
BF = jnp.bfloat16
F32 = jnp.float32


def dot(a, b, ca, cb):
    return lax.dot_general(a, b, (((ca,), (cb,)), ((), ())), preferred_element_type=F32)


def fused(
    n, norm,
    patches, taps, w_query, w_key, w_value, w_output, mask_in, cot,
    out_in, out_conv, out_q, out_k, out_v, out_o,
    mask, slabs, mixed, wq, wk, wv, wo, tp, acc, heads4, grads, plane, probs, dscores, held,
    part_out, part_in, edge_out, edge_in,
    sem_loc, sem_w, zs, zr, xs, xr, cs, cr, ps, pr, es, er,
):
    g = lax.axis_index("groups")
    b = lax.axis_index("blk")
    x = lax.axis_index("heads")
    s = lax.axis_index("sub")
    h, hx, hc, hd = x * 2 + s, (1 - x) * 2 + s, x * 2 + 1 - s, (1 - x) * 2 + 1 - s
    rows = patches.shape[0]
    wide = cot.shape[1]
    local = wide // (D // HEADS)
    hs = D // HEADS
    scale = hs ** (-0.5)
    peers = [lax.rem(b + k, n) for k in range(1, n)]
    at_peer = [(g, p, x, s) for p in peers]
    at_x, at_c, at_d = (g, b, 1 - x, s), (g, b, x, 1 - s), (g, b, 1 - x, 1 - s)

    def send(src, dst, ss, rs, where):
        c = pltpu.make_async_remote_copy(
            src_ref=src, dst_ref=dst, send_sem=ss, recv_sem=rs, device_id=where, device_id_type=MESH
        )
        c.start()
        return c

    def got(ref, sem):
        pltpu.make_async_remote_copy(
            src_ref=ref, dst_ref=ref, send_sem=sem, recv_sem=sem, device_id=at_x, device_id_type=MESH
        ).wait_recv()

    locals_ = []
    for c in range(4):
        locals_.append(
            pltpu.make_async_copy(
                patches.at[:, pl.ds(c * wide, wide)], slabs.at[b, c, 0], sem_loc.at[c]
            )
        )
    locals_.append(pltpu.make_async_copy(cot, slabs.at[b, h, 1], sem_loc.at[4]))
    locals_.append(pltpu.make_async_copy(taps, tp, sem_loc.at[5]))
    locals_.append(pltpu.make_async_copy(mask_in, mask, sem_loc.at[6]))
    weights = [
        pltpu.make_async_copy(src, dst, sem_w.at[i])
        for i, (src, dst) in enumerate(((w_query, wq), (w_key, wk), (w_value, wv), (w_output, wo)))
    ]
    for c in locals_ + weights:
        c.start()
    barrier = pltpu.get_barrier_semaphore()
    for where in at_peer + [at_x, at_c, at_d]:
        pl.semaphore_signal(barrier, inc=1, device_id=where, device_id_type=MESH)
    pl.semaphore_wait(barrier, n + 2)

    sent, relays = [], []
    own_cols = pl.ds(pl.multiple_of(h * wide, wide), wide)
    middle = lax.rem((b + 1) // 2, 2)
    inner, outer, across = b + 1 - 2 * (b // 2), middle * 3 * (b - 1), lax.rem(b + 2, n)
    last = 3 * (1 - lax.rem(b, 2))
    order = [
        inner,
        middle * last + (1 - middle) * across,
        middle * across + (1 - middle) * last,
    ]
    own_parts = (patches.at[:, own_cols], cot)

    def relay(src, t, kind, k, where):
        c = pltpu.make_async_remote_copy(
            src_ref=src, dst_ref=slabs.at[t, h, kind], send_sem=zs.at[kind, k],
            recv_sem=zr.at[kind, t], device_id=where, device_id_type=MESH,
        )
        pl.when(middle == 1)(c.start)
        relays.append(c)

    at_inner, at_outer = (g, inner, x, s), (g, outer, x, s)
    for kind in (1, 0):
        sent.append(
            send(own_parts[kind], slabs.at[b, h, kind], zs.at[kind, 0], zr.at[kind, b], at_inner)
        )
        relay(own_parts[kind], b, kind, 1, at_outer)
        if kind == 1:
            sent.append(send(cot, slabs.at[b, h, 1], xs.at[1, 0], xr.at[1, b], at_x))
            sent.append(send(cot, slabs.at[b, h, 1], cs.at[0, 1, 0], cr.at[0, 1, b], at_c))

    def from_z(k):
        p = order[k]
        for kind in (1, 0):
            part = slabs.at[p, h, kind]
            got(part, zr.at[kind, p])
            relay(part, p, kind, k + 2, at_inner if k == 1 else at_outer)
            sent.append(send(part, part, xs.at[kind, k + 1], xr.at[kind, p], at_x))
            sent.append(send(part, part, cs.at[0, kind, k + 1], cr.at[0, kind, p], at_c))

    def from_x(k):
        p = order[k] if k >= 0 else b
        for kind in (1, 0) if k >= 0 else (1,):
            part = slabs.at[p, hx, kind]
            got(part, xr.at[kind, p])
            sent.append(send(part, part, cs.at[1, kind, k + 1], cr.at[1, kind, p], at_c))

    def from_core(i, c):
        got(slabs.at[b, c, 1], cr.at[i, 1, b])
        for p in order:
            for kind in (1, 0):
                got(slabs.at[p, c, kind], cr.at[i, kind, p])

    from_z(0)
    from_x(-1)
    from_z(1)
    from_x(0)
    from_z(2)
    for c in locals_ + weights:
        c.wait()

    acc[...] = jnp.zeros_like(acc)
    row_of = lax.broadcasted_iota(jnp.int32, (n * rows, wide), 0)

    def quarter(c):
        cols = pl.ds(pl.multiple_of(c * wide, wide), wide)
        plain = slabs[:, c, 0].reshape(n * rows, wide).astype(F32)
        before = jnp.where(row_of == 0, 0.0, pltpu.roll(plain, 1, 0))
        after = jnp.where(row_of == n * rows - 1, 0.0, pltpu.roll(plain, n * rows - 1, 0))
        t = tp[:, cols]
        m = (plain + t[0:1] * before + t[1:2] * plain + t[2:3] * after).astype(BF)
        mixed[c] = m
        cq = slabs[:, c, 1].reshape(n * rows, wide)
        acc[0] += dot(m, wq[cols, :], 1, 0)
        acc[1] += dot(m, wk[cols, :], 1, 0)
        acc[2] += dot(m, wv[cols, :], 1, 0)
        acc[3] += dot(cq, wo[cols, :], 1, 0)

    quarter(h)
    from_x(1)
    from_x(2)
    from_core(0, hc)
    quarter(hc)
    quarter(hx)
    from_core(1, hd)
    quarter(hd)

    for i in range(4):
        heads4[i] = acc[i].astype(BF)

    for j in range(local):
        mine = slice(j * hs, (j + 1) * hs)
        queries, keys, values, grad = (heads4[i, :, mine] for i in (0, 1, 2, 3))
        slot = j % 2
        plane[slot, 0] = dot(queries, keys, 1, 1)
        plane[slot, 1] = dot(grad, values, 1, 1)
        inverses = []
        for i in range(n):
            here = slice(i * rows, (i + 1) * rows)
            allowed = (
                jnp.concatenate([jnp.full((rows, TILE), mask[i, t], jnp.int32) for t in range(n)], axis=1)
                == 1
            )
            score = plane[slot, 0, here] * scale
            weight = jnp.where(allowed, jnp.exp(jnp.where(allowed, score, 0.0)), 0.0)
            inverses.append(1.0 / jnp.sum(weight, -1, keepdims=True))
            plane[slot, 0, here] = weight
            probs[slot, here] = weight.astype(BF)
        att32 = dot(probs[slot], values, 1, 0) * jnp.concatenate(inverses, axis=0)
        grads[:, 3 * wide + j * hs : 3 * wide + (j + 1) * hs] = att32.astype(BF)
        delta = jnp.sum(grad.astype(F32) * att32, -1, keepdims=True)
        for i in range(n):
            here = slice(i * rows, (i + 1) * rows)
            prob = plane[slot, 0, here] * inverses[i]
            probs[slot, here] = prob.astype(BF)
            dscores[slot, here] = (prob * (plane[slot, 1, here] - delta[here]) * scale).astype(BF)
        grads[:, mine] = dot(dscores[slot], keys, 1, 0).astype(BF)
        grads[:, wide + j * hs : wide + (j + 1) * hs] = dot(
            dscores[slot], heads4[0, :, mine], 0, 0
        ).astype(BF)
        grads[:, 2 * wide + j * hs : 2 * wide + (j + 1) * hs] = dot(
            probs[slot], heads4[3, :, mine], 0, 0
        ).astype(BF)

    own_rows = pl.ds(pl.multiple_of(b * rows, rows), rows)
    grad_q = grads[own_rows, :wide]
    grad_k = grads[own_rows, wide : 2 * wide]
    grad_v = grads[own_rows, 2 * wide : 3 * wide]

    def branch(c):
        cols = pl.ds(pl.multiple_of(c * wide, wide), wide)
        return (
            dot(grad_q, wq[cols, :], 1, 1) + dot(grad_k, wk[cols, :], 1, 1)
            + dot(grad_v, wv[cols, :], 1, 1)
        )

    for k, (c, where) in enumerate(((hx, at_x), (hd, at_d), (hc, at_c))):
        part_out[k] = branch(c).astype(BF)
        sent.append(send(part_out.at[k], part_in.at[k], ps.at[k], pr.at[k], where))
    three = dot(mixed[b], grads[:, : 3 * wide], 0, 0) * norm
    for i in range(3):
        held[i] = three[:, i * wide : (i + 1) * wide]
    held[3] = dot(slabs[:, b, 1].reshape(n * rows, wide), grads[:, 3 * wide :], 0, 0) * norm
    writes = [
        pltpu.make_async_copy(held.at[i], out, sem_w.at[i])
        for i, out in enumerate((out_q, out_k, out_v, out_o))
    ]
    for c in writes:
        c.start()
    total = branch(h) + slabs[b, h, 1].astype(F32)
    for k in range(3):
        got(part_in.at[k], pr.at[k])
        total = total + part_in[k].astype(F32)

    first_row = lax.broadcasted_iota(jnp.int32, (rows, wide), 0) == 0
    last_row = lax.broadcasted_iota(jnp.int32, (rows, wide), 0) == rows - 1
    low, high = lax.rem(b + n - 1, n), lax.rem(b + 1, n)
    plain = slabs[b, h, 0].astype(F32)
    edge_low = jnp.where(b > 0, slabs[low, h, 0, rows - 16 :].astype(F32)[15:16], 0.0)
    edge_high = jnp.where(b < n - 1, slabs[high, h, 0, :16].astype(F32)[0:1], 0.0)
    before = jnp.where(first_row, edge_low, pltpu.roll(plain, 1, 0))
    after = jnp.where(last_row, edge_high, pltpu.roll(plain, rows - 1, 0))
    edge_out[0:1] = jnp.sum(total * before, 0, keepdims=True)
    edge_out[1:2] = jnp.sum(total * plain, 0, keepdims=True)
    edge_out[2:3] = jnp.sum(total * after, 0, keepdims=True)
    edge_out[3:4] = total[0:1]
    edge_out[4:5] = total[rows - 1 :]
    edge_out[5:8] = jnp.zeros((3, wide), F32)
    for k, where in enumerate(at_peer):
        sent.append(send(edge_out, edge_in.at[b], es.at[k], er.at[b], where))
    edge_in[b] = edge_out[...]

    for p in peers:
        got(edge_in.at[p], er.at[p])
    summed = edge_in[0]
    for j in range(1, n):
        summed = summed + edge_in[j]
    out_conv[...] = summed[0:3] * norm
    t = tp[:, own_cols]
    edge_low = jnp.where(b > 0, edge_in[low][4:5], 0.0)
    edge_high = jnp.where(b < n - 1, edge_in[high][3:4], 0.0)
    before = jnp.where(first_row, edge_low, pltpu.roll(total, 1, 0))
    after = jnp.where(last_row, edge_high, pltpu.roll(total, rows - 1, 0))
    out_in[...] = total * (1.0 + t[1:2]) + t[0:1] * after + t[2:3] * before
    for c in sent:
        c.wait_send()
    for c in relays:
        pl.when(middle == 1)(c.wait_send)
    for c in writes:
        c.wait()


def placed(*refs):
    ins, outs, held, sems = refs[:6], refs[6:12], refs[12:18], refs[18]
    loads = [pltpu.make_async_copy(ins[i], held[i], sems.at[0, i]) for i in range(6)]
    stores = [pltpu.make_async_copy(held[i], outs[i], sems.at[1, i]) for i in range(6)]
    for c in loads:
        c.start()
    for load, store in zip(loads, stores):
        load.wait()
        store.start()
    for c in stores:
        c.wait()


def fused_device(patches, conv_taps, w_query, w_key, w_value, w_output, tile_mask, cotangent):
    n = lax.axis_size("blk")
    rows, wide = cotangent.shape
    hs = D // HEADS
    tokens = n * rows
    dma = pltpu.SemaphoreType.DMA
    anywhere = pl.BlockSpec(memory_space=pltpu.HBM)
    vmem = pl.BlockSpec(memory_space=pltpu.VMEM)
    square = jax.ShapeDtypeStruct((D // n, wide), F32)
    shapes = (
        jax.ShapeDtypeStruct((rows, wide), F32),
        jax.ShapeDtypeStruct((3, wide), F32),
    ) + (square,) * 4
    results = pl.pallas_call(
        functools.partial(fused, n, tokens ** (-0.5)),
        out_shape=shapes,
        in_specs=[anywhere] * 8,
        out_specs=(vmem, vmem) + (anywhere,) * 4,
        scratch_shapes=[
            pltpu.SMEM((n, n), jnp.int32),
            pltpu.VMEM((n, 4, 2, rows, wide), BF),
            pltpu.VMEM((4, tokens, wide), BF),
            pltpu.VMEM((D, wide), BF),
            pltpu.VMEM((D, wide), BF),
            pltpu.VMEM((D, wide), BF),
            pltpu.VMEM((D, wide), BF),
            pltpu.VMEM((3, D), F32),
            pltpu.VMEM((4, tokens, wide), F32),
            pltpu.VMEM((4, tokens, wide), BF),
            pltpu.VMEM((tokens, 4 * wide), BF),
            pltpu.VMEM((2, 2, tokens, tokens), F32),
            pltpu.VMEM((2, tokens, tokens), BF),
            pltpu.VMEM((2, tokens, tokens), BF),
            pltpu.VMEM((4, D // n, wide), F32),
            pltpu.VMEM((3, rows, wide), BF),
            pltpu.VMEM((3, rows, wide), BF),
            pltpu.VMEM((8, wide), F32),
            pltpu.VMEM((n, 8, wide), F32),
            dma((8,)), dma((4,)),
            dma((2, n + 1)), dma((2, n)),
            dma((2, n)), dma((2, n)),
            dma((2, 2, n)), dma((2, 2, n)),
            dma((3,)), dma((3,)),
            dma((n - 1,)), dma((n,)),
        ],
        compiler_params=pltpu.CompilerParams(
            collective_id=0, has_side_effects=True, vmem_limit_bytes=60 * 1024 * 1024
        ),
    )(patches, conv_taps, w_query, w_key, w_value, w_output, tile_mask, cotangent)
    return pl.pallas_call(
        placed,
        out_shape=shapes,
        in_specs=[anywhere] * 6,
        out_specs=(anywhere,) * 6,
        scratch_shapes=[pltpu.VMEM(t.shape, F32) for t in shapes] + [dma((2, 6))],
        compiler_params=pltpu.CompilerParams(vmem_limit_bytes=60 * 1024 * 1024),
    )(*results)


def fits(mesh):
    shape = mesh.shape
    n = shape["blk"]
    return n == 4 and shape["heads"] == 2 and shape["sub"] == 2 and HEADS == 4 * n


def solution(mesh):
    in_specs = (
        P(("groups", "blk"), None),
        P(),
        P(None, ("heads", "sub")),
        P(None, ("heads", "sub")),
        P(None, ("heads", "sub")),
        P(None, ("heads", "sub")),
        P("groups", None),
        P(("groups", "blk"), ("heads", "sub")),
    )
    out_specs = (
        P(("groups", "blk"), ("heads", "sub")),
        P("groups", ("heads", "sub")),
        P(("groups", "blk"), ("heads", "sub")),
        P(("groups", "blk"), ("heads", "sub")),
        P(("groups", "blk"), ("heads", "sub")),
        P(("groups", "blk"), ("heads", "sub")),
    )
    return jax.shard_map(
        fused_device if fits(mesh) else per_device, mesh=mesh, in_specs=in_specs, out_specs=out_specs, check_vma=False
    )
```

```python
import functools

import jax
import jax.numpy as jnp
from jax import lax
from jax.experimental import pallas as pl
from jax.experimental.pallas import tpu as pltpu
from jax.sharding import PartitionSpec as P

D = 1024
HEADS = 16
TILE = 128


def padded(cells, sides, width):
    for axis, dim in sides:
        count = lax.axis_size(axis)
        ends = count - 1
        head = lax.slice_in_dim(cells, 0, width, axis=dim)
        tail = lax.slice_in_dim(cells, cells.shape[dim] - width, cells.shape[dim], axis=dim)
        cells = jnp.concatenate(
            [
                lax.ppermute(tail, axis, [(i, (i + 1) % count) for i in range(ends)]),
                cells,
                lax.ppermute(head, axis, [((i + 1) % count, i) for i in range(ends)]),
            ],
            axis=dim,
        )
    return cells


def from_behind(value, axis, steps):
    count = lax.axis_size(axis)
    pairs = [(source, (source + steps) % count) for source in range(count)]
    return lax.ppermute(value, axis, pairs)


def allowed_rows(mask_bf, first_query, query_count, first_key, key_count):
    tiles = mask_bf.shape[0]
    columns = jnp.arange(tiles, dtype=jnp.int32)
    query_tiles = (first_query + jnp.arange(query_count, dtype=jnp.int32)) // TILE
    key_tiles = (first_key + jnp.arange(key_count, dtype=jnp.int32)) // TILE
    query_hot = (query_tiles[:, None] == columns[None, :]).astype(jnp.bfloat16)
    key_hot = (key_tiles[:, None] == columns[None, :]).astype(jnp.bfloat16)
    picked = jnp.dot(query_hot, mask_bf, preferred_element_type=jnp.float32).astype(jnp.bfloat16)
    return jnp.einsum("qn,kn->qk", picked, key_hot, preferred_element_type=jnp.float32) > 0.5


def per_device(patches, conv_taps, w_query, w_key, w_value, w_output, tile_mask, cotangent):
    rows = patches.shape[0]
    local = w_query.shape[1]
    head_size = D // HEADS
    heads_here = local // head_size
    cycle_size = lax.axis_size("blk")
    position = lax.axis_index("blk")
    total_rows = rows * cycle_size
    scale = head_size ** (-0.5)
    norm = total_rows ** (-0.5)
    mask_bf = tile_mask.astype(jnp.bfloat16)
    first_query = position * rows
    padded_in = padded(patches, (("blk", 0),), 1)
    padded32 = padded_in.astype(jnp.float32)
    middle = padded32[1:-1]
    mixed = (
        middle + conv_taps[0] * padded32[:-2] + conv_taps[1] * middle + conv_taps[2] * padded32[2:]
    ).astype(jnp.bfloat16)
    queries = jnp.dot(mixed, w_query, preferred_element_type=jnp.float32).astype(jnp.bfloat16)
    keys_own = jnp.dot(mixed, w_key, preferred_element_type=jnp.float32).astype(jnp.bfloat16)
    values_own = jnp.dot(mixed, w_value, preferred_element_type=jnp.float32).astype(jnp.bfloat16)
    keys_all, values_all = (
        lax.all_gather(keys_own, "blk", axis=0, tiled=True),
        lax.all_gather(values_own, "blk", axis=0, tiled=True),
    )
    cot_full = lax.all_gather(cotangent, ("heads", "sub"), axis=1, tiled=True)
    grad_att = jnp.dot(cot_full, w_output, preferred_element_type=jnp.float32).astype(jnp.bfloat16)
    group = 1
    for power in range(12):
        if group * 2 * rows <= 1024 and cycle_size % (group * 2) == 0:
            group = group * 2
    span = group * rows
    blocks = cycle_size // group
    query_heads = queries.reshape(rows, heads_here, head_size)
    grad_heads = grad_att.reshape(rows, heads_here, head_size)
    key_blocks = keys_all.reshape(blocks, span, heads_here, head_size)
    value_blocks = values_all.reshape(blocks, span, heads_here, head_size)
    block_ids = jnp.arange(blocks, dtype=jnp.int32)

    def weights_of(key_block, allowed):
        raw = (
            jnp.einsum("qhd,khd->hqk", query_heads, key_block, preferred_element_type=jnp.float32)
            * scale
        )
        return jnp.where(allowed[None], jnp.exp(jnp.where(allowed[None], raw, 0.0)), 0.0)

    def forward_step(state, inputs):
        block_id, key_block, value_block = inputs
        allowed = allowed_rows(mask_bf, first_query, rows, block_id * span, span)
        accum, totals = state
        weights = weights_of(key_block, allowed)
        added = jnp.einsum(
            "hqk,khd->hqd",
            weights.astype(jnp.bfloat16),
            value_block,
            preferred_element_type=jnp.float32,
        )
        state = (accum + added, totals + jnp.sum(weights, -1))
        return (state, None)

    start_state = (
        jnp.zeros((heads_here, rows, head_size), jnp.float32),
        jnp.zeros((heads_here, rows), jnp.float32),
    )
    (accum, totals), unused = lax.scan(
        forward_step, start_state, (block_ids, key_blocks, value_blocks)
    )
    attended32 = accum / totals[:, :, None]
    attended = jnp.transpose(attended32, (1, 0, 2)).reshape(rows, local).astype(jnp.bfloat16)
    deltas = jnp.einsum("qhd,hqd->hq", grad_heads.astype(jnp.float32), attended32)

    def local_grads(key_block, value_block, allowed):
        weights = weights_of(key_block, allowed)
        probs = weights / totals[:, :, None]
        dprobs = jnp.einsum(
            "qhd,khd->hqk", grad_heads, value_block, preferred_element_type=jnp.float32
        )
        dscores = (probs * (dprobs - deltas[:, :, None]) * scale).astype(jnp.bfloat16)
        return (
            jnp.einsum("hqk,khd->qhd", dscores, key_block, preferred_element_type=jnp.float32),
            jnp.einsum("hqk,qhd->khd", dscores, query_heads, preferred_element_type=jnp.float32),
            jnp.einsum(
                "hqk,qhd->khd",
                probs.astype(jnp.bfloat16),
                grad_heads,
                preferred_element_type=jnp.float32,
            ),
        )

    def shard_grads(block):
        wrapped = jnp.remainder(block, cycle_size)
        key_block = lax.dynamic_slice_in_dim(keys_all, wrapped * rows, rows, 0).reshape(
            rows, heads_here, head_size
        )
        value_block = lax.dynamic_slice_in_dim(values_all, wrapped * rows, rows, 0).reshape(
            rows, heads_here, head_size
        )
        allowed = allowed_rows(mask_bf, first_query, rows, wrapped * rows, rows)
        query_add, key_term, value_term = local_grads(key_block, value_block, allowed)
        return (
            query_add,
            jnp.stack([key_term.reshape(rows, local), value_term.reshape(rows, local)]),
        )

    query_first, carried_first = shard_grads(position - 1)

    def turn(step, state):
        accum_q, carried = state
        moved = from_behind(carried, "blk", 1)
        query_add, term = shard_grads(position - step - 1)
        return (accum_q + query_add, moved + term)

    accum_q, summed = lax.fori_loop(1, cycle_size, turn, (query_first, carried_first))
    grad_keys = summed[0].astype(jnp.bfloat16)
    grad_values = summed[1].astype(jnp.bfloat16)
    grad_queries = accum_q.reshape(rows, local).astype(jnp.bfloat16)
    stacked = jnp.stack(
        [
            jnp.einsum("td,tc->dc", mixed, grad_queries, preferred_element_type=jnp.float32),
            jnp.einsum("td,tc->dc", mixed, grad_keys, preferred_element_type=jnp.float32),
            jnp.einsum("td,tc->dc", mixed, grad_values, preferred_element_type=jnp.float32),
            jnp.einsum("td,tc->dc", cot_full, attended, preferred_element_type=jnp.float32),
        ]
    )
    weight_sums = lax.psum_scatter(stacked, "blk", scatter_dimension=1, tiled=True) * norm
    partial_grad = (
        jnp.einsum("tc,dc->td", grad_queries, w_query, preferred_element_type=jnp.float32)
        + jnp.einsum("tc,dc->td", grad_keys, w_key, preferred_element_type=jnp.float32)
        + jnp.einsum("tc,dc->td", grad_values, w_value, preferred_element_type=jnp.float32)
    )
    grad_mixed = lax.psum_scatter(
        partial_grad, ("heads", "sub"), scatter_dimension=1, tiled=True
    ) + cotangent.astype(jnp.float32)
    columns_here = cotangent.shape[1]
    offset = lax.axis_index(("heads", "sub")) * columns_here
    taps_here = lax.dynamic_slice_in_dim(conv_taps, offset, columns_here, 1)
    padded_grad = padded(grad_mixed.astype(jnp.bfloat16), (("blk", 0),), 1).astype(grad_mixed.dtype)
    input_grad = (
        grad_mixed * (1.0 + taps_here[1])
        + taps_here[0] * padded_grad[2:]
        + taps_here[2] * padded_grad[:-2]
    )
    patch_cols = lax.dynamic_slice_in_dim(padded32, offset, columns_here, 1)
    conv_terms = jnp.stack(
        [
            jnp.sum(grad_mixed * patch_cols[:-2], 0),
            jnp.sum(grad_mixed * patch_cols[1:-1], 0),
            jnp.sum(grad_mixed * patch_cols[2:], 0),
        ]
    )
    conv_grad = lax.psum(conv_terms, "blk") * norm
    return (input_grad, conv_grad, weight_sums[0], weight_sums[1], weight_sums[2], weight_sums[3])

MESH = pl.DeviceIdType.MESH
BF = jnp.bfloat16
F32 = jnp.float32


def dot(a, b, ca, cb):
    return lax.dot_general(a, b, (((ca,), (cb,)), ((), ())), preferred_element_type=F32)


def fused(
    n, norm,
    patches, taps, w_query, w_key, w_value, w_output, mask_in, cot,
    out_in, out_conv, out_q, out_k, out_v, out_o,
    mask, slabs, mixed, wq, wk, wv, wo, tp, acc, heads4, grads, plane, probs, dscores, held,
    part_out, part_in, edge_out, edge_in,
    sem_loc, sem_w, zs, zr, xs, xr, cs, cr, ps, pr, es, er,
):
    g = lax.axis_index("groups")
    b = lax.axis_index("blk")
    x = lax.axis_index("heads")
    s = lax.axis_index("sub")
    h, hx, hc, hd = x * 2 + s, (1 - x) * 2 + s, x * 2 + 1 - s, (1 - x) * 2 + 1 - s
    rows = patches.shape[0]
    wide = cot.shape[1]
    local = wide // (D // HEADS)
    hs = D // HEADS
    scale = hs ** (-0.5)
    peers = [lax.rem(b + k, n) for k in range(1, n)]
    at_peer = [(g, p, x, s) for p in peers]
    at_x, at_c, at_d = (g, b, 1 - x, s), (g, b, x, 1 - s), (g, b, 1 - x, 1 - s)

    def send(src, dst, ss, rs, where):
        c = pltpu.make_async_remote_copy(
            src_ref=src, dst_ref=dst, send_sem=ss, recv_sem=rs, device_id=where, device_id_type=MESH
        )
        c.start()
        return c

    def got(ref, sem):
        pltpu.make_async_remote_copy(
            src_ref=ref, dst_ref=ref, send_sem=sem, recv_sem=sem, device_id=at_x, device_id_type=MESH
        ).wait_recv()

    locals_ = []
    for c in range(4):
        locals_.append(
            pltpu.make_async_copy(
                patches.at[:, pl.ds(c * wide, wide)], slabs.at[b, c, 0], sem_loc.at[c]
            )
        )
    locals_.append(pltpu.make_async_copy(cot, slabs.at[b, h, 1], sem_loc.at[4]))
    locals_.append(pltpu.make_async_copy(taps, tp, sem_loc.at[5]))
    locals_.append(pltpu.make_async_copy(mask_in, mask, sem_loc.at[6]))
    weights = [
        pltpu.make_async_copy(src, dst, sem_w.at[i])
        for i, (src, dst) in enumerate(((w_query, wq), (w_key, wk), (w_value, wv), (w_output, wo)))
    ]
    for c in locals_ + weights:
        c.start()
    barrier = pltpu.get_barrier_semaphore()
    for where in at_peer + [at_x, at_c, at_d]:
        pl.semaphore_signal(barrier, inc=1, device_id=where, device_id_type=MESH)
    pl.semaphore_wait(barrier, n + 2)

    sent, relays = [], []
    own_cols = pl.ds(pl.multiple_of(h * wide, wide), wide)
    middle = lax.rem((b + 1) // 2, 2)
    inner, outer, across = b + 1 - 2 * (b // 2), middle * 3 * (b - 1), lax.rem(b + 2, n)
    last = 3 * (1 - lax.rem(b, 2))
    order = [
        inner,
        middle * last + (1 - middle) * across,
        middle * across + (1 - middle) * last,
    ]
    own_parts = (patches.at[:, own_cols], cot)

    def relay(src, t, kind, k, where):
        c = pltpu.make_async_remote_copy(
            src_ref=src, dst_ref=slabs.at[t, h, kind], send_sem=zs.at[kind, k],
            recv_sem=zr.at[kind, t], device_id=where, device_id_type=MESH,
        )
        pl.when(middle == 1)(c.start)
        relays.append(c)

    at_inner, at_outer = (g, inner, x, s), (g, outer, x, s)
    for kind in (1, 0):
        sent.append(
            send(own_parts[kind], slabs.at[b, h, kind], zs.at[kind, 0], zr.at[kind, b], at_inner)
        )
        relay(own_parts[kind], b, kind, 1, at_outer)
        if kind == 1:
            sent.append(send(cot, slabs.at[b, h, 1], xs.at[1, 0], xr.at[1, b], at_x))
            sent.append(send(cot, slabs.at[b, h, 1], cs.at[0, 1, 0], cr.at[0, 1, b], at_c))

    def from_z(k):
        p = order[k]
        for kind in (1, 0):
            part = slabs.at[p, h, kind]
            got(part, zr.at[kind, p])
            relay(part, p, kind, k + 2, at_inner if k == 1 else at_outer)
            sent.append(send(part, part, xs.at[kind, k + 1], xr.at[kind, p], at_x))
            sent.append(send(part, part, cs.at[0, kind, k + 1], cr.at[0, kind, p], at_c))

    def from_x(k):
        p = order[k] if k >= 0 else b
        for kind in (1, 0) if k >= 0 else (1,):
            part = slabs.at[p, hx, kind]
            got(part, xr.at[kind, p])
            sent.append(send(part, part, cs.at[1, kind, k + 1], cr.at[1, kind, p], at_c))

    def from_core(i, c):
        got(slabs.at[b, c, 1], cr.at[i, 1, b])
        for p in order:
            for kind in (1, 0):
                got(slabs.at[p, c, kind], cr.at[i, kind, p])

    from_z(0)
    from_x(-1)
    from_z(1)
    from_x(0)
    from_z(2)
    for c in locals_ + weights:
        c.wait()

    acc[...] = jnp.zeros_like(acc)
    row_of = lax.broadcasted_iota(jnp.int32, (n * rows, wide), 0)

    def quarter(c):
        cols = pl.ds(pl.multiple_of(c * wide, wide), wide)
        plain = slabs[:, c, 0].reshape(n * rows, wide).astype(F32)
        before = jnp.where(row_of == 0, 0.0, pltpu.roll(plain, 1, 0))
        after = jnp.where(row_of == n * rows - 1, 0.0, pltpu.roll(plain, n * rows - 1, 0))
        t = tp[:, cols]
        m = (plain + t[0:1] * before + t[1:2] * plain + t[2:3] * after).astype(BF)
        mixed[c] = m
        cq = slabs[:, c, 1].reshape(n * rows, wide)
        acc[0] += dot(m, wq[cols, :], 1, 0)
        acc[1] += dot(m, wk[cols, :], 1, 0)
        acc[2] += dot(m, wv[cols, :], 1, 0)
        acc[3] += dot(cq, wo[cols, :], 1, 0)

    quarter(h)
    from_x(1)
    from_core(0, hc)
    quarter(hc)
    from_x(2)
    quarter(hx)
    from_core(1, hd)
    quarter(hd)

    for i in range(4):
        heads4[i] = acc[i].astype(BF)

    for j in range(local):
        mine = slice(j * hs, (j + 1) * hs)
        queries, keys, values, grad = (heads4[i, :, mine] for i in (0, 1, 2, 3))
        slot = j % 2
        plane[slot, 0] = dot(queries, keys, 1, 1)
        plane[slot, 1] = dot(grad, values, 1, 1)
        inverses = []
        for i in range(n):
            here = slice(i * rows, (i + 1) * rows)
            allowed = (
                jnp.concatenate([jnp.full((rows, TILE), mask[i, t], jnp.int32) for t in range(n)], axis=1)
                == 1
            )
            score = plane[slot, 0, here] * scale
            weight = jnp.where(allowed, jnp.exp(jnp.where(allowed, score, 0.0)), 0.0)
            inverses.append(1.0 / jnp.sum(weight, -1, keepdims=True))
            plane[slot, 0, here] = weight
            probs[slot, here] = weight.astype(BF)
        att32 = dot(probs[slot], values, 1, 0) * jnp.concatenate(inverses, axis=0)
        grads[:, 3 * wide + j * hs : 3 * wide + (j + 1) * hs] = att32.astype(BF)
        delta = jnp.sum(grad.astype(F32) * att32, -1, keepdims=True)
        for i in range(n):
            here = slice(i * rows, (i + 1) * rows)
            prob = plane[slot, 0, here] * inverses[i]
            probs[slot, here] = prob.astype(BF)
            dscores[slot, here] = (prob * (plane[slot, 1, here] - delta[here]) * scale).astype(BF)
        grads[:, mine] = dot(dscores[slot], keys, 1, 0).astype(BF)
        grads[:, wide + j * hs : wide + (j + 1) * hs] = dot(
            dscores[slot], heads4[0, :, mine], 0, 0
        ).astype(BF)
        grads[:, 2 * wide + j * hs : 2 * wide + (j + 1) * hs] = dot(
            probs[slot], heads4[3, :, mine], 0, 0
        ).astype(BF)

    own_rows = pl.ds(pl.multiple_of(b * rows, rows), rows)
    grad_q = grads[own_rows, :wide]
    grad_k = grads[own_rows, wide : 2 * wide]
    grad_v = grads[own_rows, 2 * wide : 3 * wide]

    def branch(c):
        cols = pl.ds(pl.multiple_of(c * wide, wide), wide)
        return (
            dot(grad_q, wq[cols, :], 1, 1) + dot(grad_k, wk[cols, :], 1, 1)
            + dot(grad_v, wv[cols, :], 1, 1)
        )

    for k, (c, where) in enumerate(((hx, at_x), (hd, at_d), (hc, at_c))):
        part_out[k] = branch(c).astype(BF)
        sent.append(send(part_out.at[k], part_in.at[k], ps.at[k], pr.at[k], where))
    three = dot(mixed[b], grads[:, : 3 * wide], 0, 0) * norm
    for i in range(3):
        held[i] = three[:, i * wide : (i + 1) * wide]
    held[3] = dot(slabs[:, b, 1].reshape(n * rows, wide), grads[:, 3 * wide :], 0, 0) * norm
    writes = [
        pltpu.make_async_copy(held.at[i], out, sem_w.at[i])
        for i, out in enumerate((out_q, out_k, out_v, out_o))
    ]
    for c in writes:
        c.start()
    total = branch(h) + slabs[b, h, 1].astype(F32)
    for k in range(3):
        got(part_in.at[k], pr.at[k])
        total = total + part_in[k].astype(F32)

    first_row = lax.broadcasted_iota(jnp.int32, (rows, wide), 0) == 0
    last_row = lax.broadcasted_iota(jnp.int32, (rows, wide), 0) == rows - 1
    low, high = lax.rem(b + n - 1, n), lax.rem(b + 1, n)
    plain = slabs[b, h, 0].astype(F32)
    edge_low = jnp.where(b > 0, slabs[low, h, 0, rows - 16 :].astype(F32)[15:16], 0.0)
    edge_high = jnp.where(b < n - 1, slabs[high, h, 0, :16].astype(F32)[0:1], 0.0)
    before = jnp.where(first_row, edge_low, pltpu.roll(plain, 1, 0))
    after = jnp.where(last_row, edge_high, pltpu.roll(plain, rows - 1, 0))
    edge_out[0:1] = jnp.sum(total * before, 0, keepdims=True)
    edge_out[1:2] = jnp.sum(total * plain, 0, keepdims=True)
    edge_out[2:3] = jnp.sum(total * after, 0, keepdims=True)
    edge_out[3:4] = total[0:1]
    edge_out[4:5] = total[rows - 1 :]
    edge_out[5:8] = jnp.zeros((3, wide), F32)
    for k, where in enumerate(at_peer):
        sent.append(send(edge_out, edge_in.at[b], es.at[k], er.at[b], where))
    edge_in[b] = edge_out[...]

    for p in peers:
        got(edge_in.at[p], er.at[p])
    summed = edge_in[0]
    for j in range(1, n):
        summed = summed + edge_in[j]
    out_conv[...] = summed[0:3] * norm
    t = tp[:, own_cols]
    edge_low = jnp.where(b > 0, edge_in[low][4:5], 0.0)
    edge_high = jnp.where(b < n - 1, edge_in[high][3:4], 0.0)
    before = jnp.where(first_row, edge_low, pltpu.roll(total, 1, 0))
    after = jnp.where(last_row, edge_high, pltpu.roll(total, rows - 1, 0))
    out_in[...] = total * (1.0 + t[1:2]) + t[0:1] * after + t[2:3] * before
    for c in sent:
        c.wait_send()
    for c in relays:
        pl.when(middle == 1)(c.wait_send)
    for c in writes:
        c.wait()


def placed(*refs):
    ins, outs, held, sems = refs[:6], refs[6:12], refs[12:18], refs[18]
    loads = [pltpu.make_async_copy(ins[i], held[i], sems.at[0, i]) for i in range(6)]
    stores = [pltpu.make_async_copy(held[i], outs[i], sems.at[1, i]) for i in range(6)]
    for c in loads:
        c.start()
    for load, store in zip(loads, stores):
        load.wait()
        store.start()
    for c in stores:
        c.wait()


def fused_device(patches, conv_taps, w_query, w_key, w_value, w_output, tile_mask, cotangent):
    n = lax.axis_size("blk")
    rows, wide = cotangent.shape
    hs = D // HEADS
    tokens = n * rows
    dma = pltpu.SemaphoreType.DMA
    anywhere = pl.BlockSpec(memory_space=pltpu.HBM)
    vmem = pl.BlockSpec(memory_space=pltpu.VMEM)
    square = jax.ShapeDtypeStruct((D // n, wide), F32)
    shapes = (
        jax.ShapeDtypeStruct((rows, wide), F32),
        jax.ShapeDtypeStruct((3, wide), F32),
    ) + (square,) * 4
    results = pl.pallas_call(
        functools.partial(fused, n, tokens ** (-0.5)),
        out_shape=shapes,
        in_specs=[anywhere] * 8,
        out_specs=(vmem, vmem) + (anywhere,) * 4,
        scratch_shapes=[
            pltpu.SMEM((n, n), jnp.int32),
            pltpu.VMEM((n, 4, 2, rows, wide), BF),
            pltpu.VMEM((4, tokens, wide), BF),
            pltpu.VMEM((D, wide), BF),
            pltpu.VMEM((D, wide), BF),
            pltpu.VMEM((D, wide), BF),
            pltpu.VMEM((D, wide), BF),
            pltpu.VMEM((3, D), F32),
            pltpu.VMEM((4, tokens, wide), F32),
            pltpu.VMEM((4, tokens, wide), BF),
            pltpu.VMEM((tokens, 4 * wide), BF),
            pltpu.VMEM((2, 2, tokens, tokens), F32),
            pltpu.VMEM((2, tokens, tokens), BF),
            pltpu.VMEM((2, tokens, tokens), BF),
            pltpu.VMEM((4, D // n, wide), F32),
            pltpu.VMEM((3, rows, wide), BF),
            pltpu.VMEM((3, rows, wide), BF),
            pltpu.VMEM((8, wide), F32),
            pltpu.VMEM((n, 8, wide), F32),
            dma((8,)), dma((4,)),
            dma((2, n + 1)), dma((2, n)),
            dma((2, n)), dma((2, n)),
            dma((2, 2, n)), dma((2, 2, n)),
            dma((3,)), dma((3,)),
            dma((n - 1,)), dma((n,)),
        ],
        compiler_params=pltpu.CompilerParams(
            collective_id=0, has_side_effects=True, vmem_limit_bytes=60 * 1024 * 1024
        ),
    )(patches, conv_taps, w_query, w_key, w_value, w_output, tile_mask, cotangent)
    return pl.pallas_call(
        placed,
        out_shape=shapes,
        in_specs=[anywhere] * 6,
        out_specs=(anywhere,) * 6,
        scratch_shapes=[pltpu.VMEM(t.shape, F32) for t in shapes] + [dma((2, 6))],
        compiler_params=pltpu.CompilerParams(vmem_limit_bytes=60 * 1024 * 1024),
    )(*results)


def fits(mesh):
    shape = mesh.shape
    n = shape["blk"]
    return n == 4 and shape["heads"] == 2 and shape["sub"] == 2 and HEADS == 4 * n


def solution(mesh):
    in_specs = (
        P(("groups", "blk"), None),
        P(),
        P(None, ("heads", "sub")),
        P(None, ("heads", "sub")),
        P(None, ("heads", "sub")),
        P(None, ("heads", "sub")),
        P("groups", None),
        P(("groups", "blk"), ("heads", "sub")),
    )
    out_specs = (
        P(("groups", "blk"), ("heads", "sub")),
        P("groups", ("heads", "sub")),
        P(("groups", "blk"), ("heads", "sub")),
        P(("groups", "blk"), ("heads", "sub")),
        P(("groups", "blk"), ("heads", "sub")),
        P(("groups", "blk"), ("heads", "sub")),
    )
    return jax.shard_map(
        fused_device if fits(mesh) else per_device, mesh=mesh, in_specs=in_specs, out_specs=out_specs, check_vma=False
    )
```
